128 devices in a mesh: seq: 16 (over z, y), chan: 8 (over x, core).
Axes of the slice: x: 4, y: 4, z: 4, core: 2. Of those that a mesh axis runs over, the one named last changes fastest.
Arguments:
- gate_query: bfloat16 [24576, 4096], P('seq', 'chan'), may hold values from -6 to 6
- key_proj: bfloat16 [24576, 4096], P('seq', 'chan'), may hold values from -6 to 6
- value_proj: bfloat16 [24576, 4096], P('seq', 'chan'), may hold values from -6 to 6
- decay_rates: float32 [16, 4096], P(None, 'chan'), may hold values from 0 to 1, as said below
- residues: float32 [16, 4096], P(None, 'chan'), may hold values from -1.5 to 1.5
- skip_weight: float32 [4096], P('chan'), may hold values from -6 to 6
- out_weight: bfloat16 [4096, 4096], P(None, 'chan'), may hold values from -0.09375 to 0.09375
Outputs:
- mixed: bfloat16 [24576, 4096], P('seq', 'chan')
The draws below stay inside these ranges and needn't reach their ends.
Inputs may be any that keep to these rules, and one draw needn't show every extreme that they name: `decay_rates`: decay rates are positive and at most 1/8.
All inputs are finite; a program needn't handle non-finite values.
Results may differ from the reference program's by a relative error of at most 0.0049.
Values may be sent and summed in bfloat16 or wider, within the bound.
No kernel may reach another device: no remote copies, remote signals or barrier semaphores. Data moves between devices by JAX's collectives and lax.ppermute only.
A program may use at most 256 MiB of HBM per device.

```python
import math
import jax
import jax.numpy as jnp
from jax import lax

D = 4096
MODES = 16
TOKENS = 24576


def draw_decay_rates(key, part):
    key = jax.random.fold_in(key, 7)
    slow_key, fast_key, pick_key = jax.random.split(key, 3)
    extent = (MODES, D)
    slower = jnp.exp(jax.random.uniform(slow_key, extent, jnp.float32, math.log(0.1 / TOKENS), math.log(2.0 / TOKENS)))
    faster = jnp.exp(jax.random.uniform(fast_key, extent, jnp.float32, math.log(1.0 / 50.0), math.log(0.125)))
    portion = 0.5
    return jnp.where(jax.random.uniform(pick_key, extent, jnp.float32) < portion, slower, faster)


def level_of(key, dims, cuts, low, largest):
    gain, own = 1.0, jax.random.fold_in(key, 6)
    for dim, shards_of in cuts:
        draws = jnp.exp(jax.random.uniform(jax.random.fold_in(own, dim), (shards_of,), jnp.float32, low / len(cuts), largest / len(cuts)))
        gain = gain * jnp.repeat(draws, dims[dim] // shards_of).reshape([-1 if axis == dim else 1 for axis in range(len(dims))])
    return gain


def gaussian(stream_key, shape, spread, bound, cuts=(), kind=jnp.bfloat16):
    values = spread * jax.random.normal(stream_key, shape, jnp.float32)
    if cuts:
        values = values * level_of(stream_key, shape, cuts, -0.22, 0.18)
    return jnp.clip(values, -bound, bound).astype(kind)


def setup_inputs(seed: int = 0) -> dict:
    key_of = jax.random.split(jax.random.key(seed), 8)
    gate_query = gaussian(key_of[0], (TOKENS, D), 1.0, 6.0, ((0, 16), (1, 8)))
    key_proj = gaussian(key_of[1], (TOKENS, D), 1.0, 6.0, ((0, 16), (1, 8)))
    value_proj = gaussian(key_of[2], (TOKENS, D), 1.0, 6.0, ((0, 16), (1, 8)))
    decay_rates = draw_decay_rates(jax.random.fold_in(key_of[7], 71), 0)
    residues = gaussian(key_of[4], (MODES, D), 0.25, 1.5, ((1, 8),), jnp.float32)
    skip_weight = gaussian(key_of[5], (D,), 1.0, 6.0, ((0, 8),), jnp.float32)
    out_weight = gaussian(key_of[6], (D, D), D ** -0.5, 0.09375, ((1, 8),))
    return dict(gate_query=gate_query, key_proj=key_proj, value_proj=value_proj, decay_rates=decay_rates, residues=residues, skip_weight=skip_weight, out_weight=out_weight)


block_span = 128
channel_group = 128

def filter_tables(chan_rate, chan_residue):
    highest = lax.Precision.HIGHEST
    mode_gain = chan_residue * jnp.sqrt(-jnp.expm1(-2.0 * chan_rate))
    offsets = jnp.arange(block_span).astype(jnp.float32)
    powers = jnp.exp(-chan_rate[:, :, None] * offsets)
    impulse = jnp.einsum('cm,cmt->ct', mode_gain, powers, precision=highest)
    lag_grid = jnp.arange(block_span)[:, None] - jnp.arange(block_span)[None, :]
    toeplitz = jnp.where(lag_grid >= 0, impulse[:, jnp.clip(lag_grid, 0, block_span - 1)], 0.0)
    ending = powers[:, :, ::-1]
    reading = mode_gain[:, :, None] * powers * jnp.exp(-chan_rate)[:, :, None]
    stride = jnp.exp(-chan_rate * block_span)
    return (toeplitz, ending, reading, stride)

def local_pass(inputs_cf, tables):
    highest = lax.Precision.HIGHEST
    toeplitz, ending, reading, stride = tables
    within = jnp.einsum('cij,cnj->cni', toeplitz, inputs_cf, precision=highest)
    sealed = jnp.einsum('cmj,cnj->ncm', ending, inputs_cf, precision=highest)

    def advance(state_now, sealed_one):
        return (stride * state_now + sealed_one, state_now)
    closing, entries = lax.scan(advance, jnp.zeros(stride.shape, jnp.float32), sealed)
    return (within, entries, closing)

def state_output(reading, entries):
    return jnp.einsum('cmi,ncm->cni', reading, entries, precision=lax.Precision.HIGHEST)

def reference(gate_query, key_proj, value_proj, decay_rates, residues, skip_weight, out_weight):
    product = key_proj.astype(jnp.float32) * value_proj.astype(jnp.float32)
    groups_total = D // channel_group

    def one_group(group_id):
        offset = (group_id * channel_group).astype(jnp.int32)
        columns = lax.dynamic_slice_in_dim(product, offset, channel_group, 1)
        chan_rate = lax.dynamic_slice_in_dim(decay_rates, offset, channel_group, 1).T
        chan_residue = lax.dynamic_slice_in_dim(residues, offset, channel_group, 1).T
        skip_gain = lax.dynamic_slice_in_dim(skip_weight, offset, channel_group, 0)
        tables = filter_tables(chan_rate, chan_residue)
        inputs_cf = columns.T.reshape(channel_group, TOKENS // block_span, block_span)
        within, entries, closing = local_pass(inputs_cf, tables)
        result = within + state_output(tables[2], entries) + skip_gain[:, None, None] * inputs_cf
        return result.reshape(channel_group, TOKENS)
    convolved = lax.map(one_group, jnp.arange(groups_total, dtype=jnp.int32))
    convolved = convolved.reshape(D, TOKENS).T
    gated = (gate_query.astype(jnp.float32) * convolved).astype(jnp.bfloat16)
    return jnp.dot(gated, out_weight, preferred_element_type=jnp.float32).astype(jnp.bfloat16)
```

```python
import functools

import jax
import jax.numpy as jnp
from jax import lax
from jax.experimental import pallas as pl
from jax.experimental.pallas import tpu as pltpu
from jax.sharding import PartitionSpec as P

SEGS = 8
LANES = 128


def rows_of(value):
    return jnp.broadcast_to(value, (SEGS, LANES))


def closing_kernel(k_ref, v_ref, rate_ref, p_ref, entry_ref, closing_ref, flat_ref):
    modes = rate_ref.shape[0]
    steps = p_ref.shape[0]
    tile = 64

    def multiply(i, carry):
        rows = pl.ds(pl.multiple_of(i * tile, tile), tile)
        flat_ref[rows, :] = k_ref[rows, :].astype(jnp.float32) * v_ref[rows, :].astype(jnp.float32)
        return carry

    lax.fori_loop(0, flat_ref.shape[0] // tile, multiply, 0, unroll=2)
    rate = rate_ref[...]
    pole = jnp.exp(-rate)
    poles = [rows_of(pole[m : m + 1, :]) for m in range(modes)]

    def step(t, states):
        x = flat_ref[pl.ds(t, SEGS, stride=steps), :]
        p_ref[t] = x
        return tuple(a * s + x for a, s in zip(poles, states))

    zero = jnp.zeros((SEGS, LANES), jnp.float32)
    states = lax.fori_loop(0, steps, step, (zero,) * modes, unroll=8)
    segment = lax.broadcasted_iota(jnp.int32, (SEGS, LANES), 0)
    for m in range(modes):
        total = states[m]
        for hop in (1, 2, 4):
            decay = rows_of(jnp.exp(-rate[m : m + 1, :] * (steps * hop)))
            moved = jnp.where(segment >= hop, pltpu.roll(total, hop, 0), 0.0)
            total = total + decay * moved
        entry_ref[m] = jnp.where(segment >= 1, pltpu.roll(total, 1, 0), 0.0)
        closing_ref[m : m + 1, :] = total[SEGS - 1 :, :]


def closing_pass(k, v, rate):
    rows, width = k.shape
    modes = rate.shape[0]
    steps = rows // SEGS
    col = lambda c: (0, c)
    deep = lambda c: (0, 0, c)
    return pl.pallas_call(
        closing_kernel,
        grid=(width // LANES,),
        in_specs=[
            pl.BlockSpec((rows, LANES), col),
            pl.BlockSpec((rows, LANES), col),
            pl.BlockSpec((modes, LANES), col),
        ],
        out_specs=[
            pl.BlockSpec((steps, SEGS, LANES), deep),
            pl.BlockSpec((modes, SEGS, LANES), deep),
            pl.BlockSpec((modes, LANES), col),
        ],
        out_shape=[
            jax.ShapeDtypeStruct((steps, SEGS, width), jnp.float32),
            jax.ShapeDtypeStruct((modes, SEGS, width), jnp.float32),
            jax.ShapeDtypeStruct((modes, width), jnp.float32),
        ],
        scratch_shapes=[pltpu.VMEM((rows, LANES), jnp.float32)],
        name="closing_pass",
    )(k, v, rate)


def gate_kernel(first, steps_all, p_ref, q_ref, rate_ref, gain_ref, skip_ref, *rest):
    if first:
        arriving_ref, entry_ref, gated_ref, after_ref, flat_ref = rest
    else:
        entry_ref, gated_ref, after_ref, flat_ref = rest
    modes = rate_ref.shape[0]
    steps = p_ref.shape[0]
    rate = rate_ref[...]
    pole = jnp.exp(-rate)
    poles = [rows_of(pole[m : m + 1, :]) for m in range(modes)]
    gains = [rows_of(gain_ref[m : m + 1, :]) for m in range(modes)]
    skip = rows_of(skip_ref[...])
    states = [entry_ref[m] for m in range(modes)]
    if first:
        segment = lax.broadcasted_iota(jnp.int32, (SEGS, LANES), 0)
        ahead = (segment * steps_all).astype(jnp.float32)
        states = [
            s + jnp.exp(-rate[m : m + 1, :] * ahead) * arriving_ref[m : m + 1, :]
            for m, s in enumerate(states)
        ]

    def step(t, states):
        x = p_ref[t]
        states = tuple(a * s + x for a, s in zip(poles, states))
        terms = [g * s for g, s in zip(gains, states)] + [skip * x]
        while len(terms) > 1:
            terms = [sum(terms[i : i + 2][1:], terms[i]) for i in range(0, len(terms), 2)]
        flat_ref[pl.ds(t, SEGS, stride=steps), :] = terms[0]
        return states

    states = lax.fori_loop(0, steps, step, tuple(states), unroll=8)
    for m in range(modes):
        after_ref[m] = states[m]
    for s in range(SEGS):
        y = flat_ref[s * steps : (s + 1) * steps, :]
        gated_ref[s] = (q_ref[s].astype(jnp.float32) * y).astype(jnp.bfloat16)


def gate_pass(p, q, rate, gain, skip, entry, arriving, part, parts):
    steps_all, segs, width = p.shape
    modes = rate.shape[0]
    steps = steps_all // parts
    first = arriving is not None
    col = lambda c: (0, c)
    deep = lambda c: (0, 0, c)
    in_specs = [
        pl.BlockSpec((steps, SEGS, LANES), lambda c: (part, 0, c)),
        pl.BlockSpec((SEGS, steps, LANES), lambda c: (0, part, c)),
        pl.BlockSpec((modes, LANES), col),
        pl.BlockSpec((modes, LANES), col),
        pl.BlockSpec((1, LANES), col),
    ]
    args = [p, q.reshape(SEGS, steps_all, width), rate, gain, skip.reshape(1, width)]
    if first:
        in_specs.append(pl.BlockSpec((modes, LANES), col))
        args.append(arriving)
    in_specs.append(pl.BlockSpec((modes, SEGS, LANES), deep))
    args.append(entry)
    return pl.pallas_call(
        functools.partial(gate_kernel, first, steps_all),
        grid=(width // LANES,),
        in_specs=in_specs,
        out_specs=[
            pl.BlockSpec((SEGS, steps, LANES), deep),
            pl.BlockSpec((modes, SEGS, LANES), deep),
        ],
        out_shape=[
            jax.ShapeDtypeStruct((SEGS, steps, width), jnp.bfloat16),
            jax.ShapeDtypeStruct((modes, SEGS, width), jnp.float32),
        ],
        scratch_shapes=[pltpu.VMEM((SEGS * steps, LANES), jnp.float32)],
        name="gate_pass",
    )(*args)


def partial_kernel(slot_ref, *refs):
    blocks, weights, out_ref = refs[:4], refs[4:8], refs[8]
    total = None
    for block, weight in zip(blocks, weights):
        term = jnp.dot(block[...], weight[0], preferred_element_type=jnp.float32)
        total = term if total is None else total + term
    out_ref[...] = total.astype(out_ref.dtype)


def partial_product(blocks, weight, slots):
    rows, depth = blocks[0].shape
    width = weight.shape[2]
    tile = 256
    whole = pl.BlockSpec((rows, depth), lambda n, slot: (0, 0))
    return pl.pallas_call(
        partial_kernel,
        grid_spec=pltpu.PrefetchScalarGridSpec(
            num_scalar_prefetch=1,
            grid=(width // tile,),
            in_specs=[whole] * 4
            + [
                pl.BlockSpec((1, depth, tile), lambda n, slot, k=k: (slot[k], 0, n))
                for k in range(4)
            ],
            out_specs=pl.BlockSpec((rows, tile), lambda n, slot: (0, n)),
        ),
        out_shape=jax.ShapeDtypeStruct((rows, width), jnp.bfloat16),
        name="partial_product",
    )(slots, *blocks, *([weight] * 4))


def finish_kernel(slot_ref, *refs):
    blocks, weights, other_ref, out_ref = refs[:4], refs[4:8], refs[8], refs[-1]
    total = other_ref[...].astype(jnp.float32)
    for block, weight in zip(blocks, weights):
        total = total + jnp.dot(block[...], weight[0], preferred_element_type=jnp.float32)
    out_ref[...] = total.astype(out_ref.dtype).reshape(out_ref.shape)


def finish_product(blocks, weight, slots, other, out, part, steps_all):
    rows, depth = blocks[0].shape
    width = weight.shape[2]
    steps = rows // SEGS
    tile = 256
    whole = pl.BlockSpec((rows, depth), lambda n, slot: (0, 0))
    in_specs = (
        [whole] * 4
        + [
            pl.BlockSpec((1, depth, tile), lambda n, slot, k=k: (slot[k], 0, n)) for k in range(4)
        ]
        + [pl.BlockSpec((rows, tile), lambda n, slot: (0, n))]
    )
    args = [slots, *blocks, *([weight] * 4), other]
    aliases = {}
    if out is not None:
        in_specs.append(pl.BlockSpec(memory_space=pl.ANY))
        args.append(out)
        aliases = {len(args) - 1: 0}
    return pl.pallas_call(
        finish_kernel,
        grid_spec=pltpu.PrefetchScalarGridSpec(
            num_scalar_prefetch=1,
            grid=(width // tile,),
            in_specs=in_specs,
            out_specs=pl.BlockSpec((SEGS, steps, tile), lambda n, slot: (0, part, n)),
        ),
        out_shape=jax.ShapeDtypeStruct((SEGS, steps_all, width), jnp.bfloat16),
        input_output_aliases=aliases,
        name="finish_product",
    )(*args)


def to_chan(value, target):
    return lax.ppermute(value, "chan", [(i, target(i)) for i in range(8)])


def flip_chip(i):
    return i ^ 2


def flip_core(i):
    return i ^ 1


def facing_chip(i):
    return 2 * (3 - i // 2) + i % 2


def along_y(value, by):
    return lax.ppermute(
        value, "seq", [(s, s // 4 * 4 + (s % 4 + by) % 4) for s in range(16)]
    )


def along_z(value, by):
    return lax.ppermute(value, "seq", [(s, s + 4 * by) for s in range(16) if s + 4 * by < 16])


def arriving_state(closing, rate, block_rows):
    place = lax.axis_index("seq")
    y = place % 4
    decay = lambda blocks: jnp.exp(-rate * jnp.asarray(block_rows * blocks).astype(jnp.float32))
    near = [closing] + [along_y(closing, by) for by in (1, 2, 3)]
    ahead = jnp.zeros_like(closing)
    total = jnp.zeros_like(closing)
    for by, value in enumerate(near):
        source = (y - by) % 4
        total = total + decay(3 - source) * value
        if by:
            ahead = ahead + jnp.where(source < y, decay(y - 1 - source), 0.0) * value
    far = jnp.zeros_like(closing)
    for by in (1, 2, 3):
        far = far + decay(jnp.asarray(4 * (by - 1))) * along_z(total, by)
    return ahead + decay(y) * far


PARTS = 4


def shards(gate_query, key_proj, value_proj, decay_rates, residues, skip_weight, out_weight):
    rows_here, width_here = key_proj.shape
    steps_all = rows_here // SEGS
    chan = lax.axis_index("chan")
    chip, core = chan // 2, chan % 2
    y = lax.axis_index("seq") % 4

    def wanted(chip, core):
        return [
            2 * chip + core,
            2 * (chip ^ 1) + core,
            2 * chip + (1 - core),
            2 * (chip ^ 1) + (1 - core),
        ]

    weight = out_weight.reshape(8, width_here, width_here)
    facing = jnp.stack(wanted(3 - chip, core))
    own_quarter = lax.dynamic_index_in_dim(weight, facing[y], 0, keepdims=False)
    quarter = to_chan(own_quarter, facing_chip)

    p, entry, closing = closing_pass(key_proj, value_proj, decay_rates)
    arriving = arriving_state(closing, decay_rates, rows_here)
    gain = residues * jnp.sqrt(-jnp.expm1(-2.0 * decay_rates))

    facing_weight = jnp.stack([quarter] + [along_y(quarter, by) for by in (1, 2, 3)])
    facing_slots = ((y - jnp.arange(4)) % 4).astype(jnp.int32)
    own_slots = jnp.stack(wanted(chip, core)).astype(jnp.int32)

    state = entry
    out = None
    held = []
    for part in range(PARTS):
        gated, state = gate_pass(
            p, gate_query, decay_rates, gain, skip_weight, state,
            arriving if part == 0 else None, part, PARTS,
        )
        gated = gated.reshape(rows_here // PARTS, width_here)
        near = to_chan(gated, flip_chip)
        blocks = [gated, near, to_chan(gated, flip_core), to_chan(near, flip_core)]
        partial = partial_product(blocks, facing_weight, facing_slots)
        held.append((blocks, to_chan(partial, facing_chip)))
    for part, (blocks, other) in enumerate(held):
        out = finish_product(blocks, weight, own_slots, other, out, part, steps_all)
    return out.reshape(rows_here, width_here)


def solution(mesh):
    in_specs = (
        P("seq", "chan"),
        P("seq", "chan"),
        P("seq", "chan"),
        P(None, "chan"),
        P(None, "chan"),
        P("chan"),
        P(None, "chan"),
    )
    out_specs = P("seq", "chan")
    return jax.shard_map(shards, mesh=mesh, in_specs=in_specs, out_specs=out_specs, check_vma=False)
```

```python
import functools

import jax
import jax.numpy as jnp
from jax import lax
from jax.experimental import pallas as pl
from jax.experimental.pallas import tpu as pltpu
from jax.sharding import PartitionSpec as P

SEGS = 8
LANES = 128
LOADS = 4
IN_VMEM = pl.BlockSpec(memory_space=pltpu.VMEM)
IN_SMEM = pl.BlockSpec(memory_space=pltpu.SMEM)
IN_PLACE = pl.BlockSpec(memory_space=pl.ANY)
IN_HBM = pl.BlockSpec(memory_space=pltpu.HBM)


def params(mebibytes=8):
    return pltpu.CompilerParams(vmem_limit_bytes=mebibytes << 20)


def in_hbm(value):
    return pltpu.with_memory_space_constraint(value, pltpu.HBM)


def cost(microseconds):
    return pl.CostEstimate(flops=int(microseconds * 1.15e9), bytes_accessed=0, transcendentals=0)


def spread(row):
    return jnp.broadcast_to(row, (SEGS, LANES))


def tiles(width):
    return [slice(at, at + LANES) for at in range(0, width, LANES)]


def closing_kernel(
    k_hbm, v_hbm, rate_ref, p_ref, entry_ref, closing_ref, k_buf, v_buf, flat_ref, state_ref, sems
):
    modes, width = rate_ref.shape
    steps = p_ref.shape[0]
    span = steps // LOADS
    stride = span + 1
    copies = []
    for i in range(LOADS):
        here = pl.ds(i * span, span)
        pair = [
            pltpu.make_async_copy(src.at[:, here, :], buf.at[i], sems.at[which, i])
            for which, (src, buf) in enumerate(((k_hbm, k_buf), (v_hbm, v_buf)))
        ]
        for copy in pair:
            copy.start()
        copies.append(pair)
    rate = rate_ref[...]
    pole = jnp.exp(-rate)
    for i in range(LOADS):
        for copy in copies[i]:
            copy.wait()
        for cols in tiles(width):
            for s in range(SEGS):
                flat_ref[s * stride : s * stride + span, :] = k_buf[i, s, :, cols].astype(
                    jnp.float32
                ) * v_buf[i, s, :, cols].astype(jnp.float32)
            poles = [spread(pole[m : m + 1, cols]) for m in range(modes)]

            def step(t, states):
                x = flat_ref[pl.ds(t, SEGS, stride=stride), :]
                p_ref[i * span + t, :, cols] = x
                return tuple(a * s + x for a, s in zip(poles, states))

            if i == 0:
                states = (jnp.zeros((SEGS, LANES), jnp.float32),) * modes
            else:
                states = tuple(state_ref[m, :, cols] for m in range(modes))
            states = lax.fori_loop(0, span, step, states, unroll=UNROLL_CLOSING)
            for m in range(modes):
                state_ref[m, :, cols] = states[m]
    once = jnp.exp(-rate * steps)
    twice = once * once
    hops = ((1, once), (2, twice), (4, twice * twice))
    segment = lax.broadcasted_iota(jnp.int32, (SEGS, LANES), 0)
    for cols in tiles(width):
        for m in range(modes):
            total = state_ref[m, :, cols]
            for hop, decay in hops:
                moved = jnp.where(segment >= hop, pltpu.roll(total, hop, 0), 0.0)
                total = total + spread(decay[m : m + 1, cols]) * moved
            entry_ref[m, :, cols] = jnp.where(segment >= 1, pltpu.roll(total, 1, 0), 0.0)
            closing_ref[m : m + 1, cols] = total[SEGS - 1 :, :]


UNROLL_CLOSING = 16
CLOSING_GRANT = 32
CLOSING_US = 5.5
GATE_US = 0.3
UNROLL_GATE = 4


def closing_pass(k, v, rate):
    rows, width = k.shape
    modes = rate.shape[0]
    steps = rows // SEGS
    span = steps // LOADS
    buffer = pltpu.VMEM((LOADS, SEGS, span, width), k.dtype)
    return pl.pallas_call(
        closing_kernel,
        in_specs=[IN_HBM, IN_HBM, IN_VMEM],
        out_specs=[IN_VMEM] * 3,
        out_shape=[
            jax.ShapeDtypeStruct((steps, SEGS, width), jnp.float32),
            jax.ShapeDtypeStruct((modes, SEGS, width), jnp.float32),
            jax.ShapeDtypeStruct((modes, width), jnp.float32),
        ],
        scratch_shapes=[
            buffer,
            buffer,
            pltpu.VMEM((SEGS * (span + 1), LANES), jnp.float32),
            pltpu.VMEM((modes, SEGS, width), jnp.float32),
            pltpu.SemaphoreType.DMA((2, LOADS)),
        ],
        compiler_params=params(CLOSING_GRANT),
        cost_estimate=cost(CLOSING_US),
        name="closing_pass",
    )(in_hbm(k.reshape(SEGS, steps, width)), in_hbm(v.reshape(SEGS, steps, width)), rate)


def gate_kernel(first, waits, offset, p_ref, q_hbm, rate_ref, gain_ref, skip_ref, *rest):
    arriving_ref = rest[0]
    entry_ref = rest[int(first)]
    gated_ref, after_ref, flat_ref, q_buf, sem = rest[int(first) + 1 + waits :]
    modes, width = rate_ref.shape
    steps = gated_ref.shape[1]
    stride = steps + 1
    fetch = pltpu.make_async_copy(q_hbm.at[:, pl.ds(offset, steps), :], q_buf, sem)
    fetch.start()
    rate = rate_ref[...]
    pole = jnp.exp(-rate)
    if first:
        once = jnp.exp(-rate * p_ref.shape[0])
        twice = once * once
        fourth = twice * twice
        segment = lax.broadcasted_iota(jnp.int32, (SEGS, LANES), 0)
        odd, upper, top = (segment % 2 >= 1, segment % 4 >= 2, segment >= 4)
    for at, cols in enumerate(tiles(width)):
        poles = [spread(pole[m : m + 1, cols]) for m in range(modes)]
        gains = [spread(gain_ref[m : m + 1, cols]) for m in range(modes)]
        skip = spread(skip_ref[:, cols])
        states = []
        for m in range(modes):
            state = entry_ref[m, :, cols]
            if first:
                carried = spread(arriving_ref[m : m + 1, cols])
                for picked, decay in ((odd, once), (upper, twice), (top, fourth)):
                    carried = jnp.where(picked, carried * spread(decay[m : m + 1, cols]), carried)
                state = state + carried
            states.append(state)

        def step(t, states):
            x = p_ref[offset + t, :, cols]
            states = tuple(a * s + x for a, s in zip(poles, states))
            terms = [g * s for g, s in zip(gains, states)] + [skip * x]
            while len(terms) > 1:
                terms = [
                    terms[i] + terms[i + 1] if i + 1 < len(terms) else terms[i]
                    for i in range(0, len(terms), 2)
                ]
            flat_ref[at, pl.ds(t, SEGS, stride=stride), :] = terms[0]
            return states

        states = lax.fori_loop(0, steps, step, tuple(states), unroll=UNROLL_GATE)
        for m in range(modes):
            after_ref[m, :, cols] = states[m]
    fetch.wait()
    for at, cols in enumerate(tiles(width)):
        for s in range(SEGS):
            y = flat_ref[at, s * stride : s * stride + steps, :]
            q = q_buf[s, :, cols].astype(jnp.float32)
            gated_ref[s, :, cols] = (q * y).astype(jnp.bfloat16)


def gate_pass(p, q, rate, gain, skip, entry, arriving, offset, steps, after):
    steps_all, segs, width = p.shape
    modes = rate.shape[0]
    first = arriving is not None
    args = [p, in_hbm(q.reshape(SEGS, steps_all, width)), rate, gain, skip.reshape(1, width)]
    args += ([arriving] if first else []) + [entry]
    in_specs = [IN_VMEM] * len(args) + [IN_PLACE] * len(after)
    in_specs[1] = IN_HBM
    return pl.pallas_call(
        functools.partial(gate_kernel, first, len(after), offset),
        in_specs=in_specs,
        out_specs=[IN_VMEM] * 2,
        out_shape=[
            jax.ShapeDtypeStruct((SEGS, steps, width), jnp.bfloat16),
            jax.ShapeDtypeStruct((modes, SEGS, width), jnp.float32),
        ],
        scratch_shapes=[
            pltpu.VMEM((width // LANES, SEGS * (steps + 1), LANES), jnp.float32),
            pltpu.VMEM((SEGS, steps, width), q.dtype),
            pltpu.SemaphoreType.DMA,
        ],
        compiler_params=params(),
        cost_estimate=cost(GATE_US),
        name="gate_pass",
    )(*args, *after)


def stack_kernel(place_ref, *refs):
    pieces, out_ref = refs[:-1], refs[-1]
    for i, piece in enumerate(pieces):
        out_ref[place_ref[2 + i]] = piece[...]


def stack_blocks(place, pieces):
    return pl.pallas_call(
        stack_kernel,
        in_specs=[IN_SMEM] + [IN_VMEM] * len(pieces),
        out_specs=IN_VMEM,
        out_shape=jax.ShapeDtypeStruct((len(pieces),) + pieces[0].shape, pieces[0].dtype),
        compiler_params=params(),
        name="stack_blocks",
    )(place, *pieces)


def project_kernel(place_ref, *refs):
    blocks, facing_ref, weight_hbm = refs[:4], refs[4], refs[5]
    send_ref, own_ref, weight_buf, sems = refs[-4:]
    fetches = [
        pltpu.make_async_copy(weight_hbm.at[place_ref[6 + k]], weight_buf.at[k], sems.at[k])
        for k in range(4)
    ]
    for fetch in fetches:
        fetch.start()
    total = jnp.dot(blocks[0][...], facing_ref[0], preferred_element_type=jnp.float32)
    for k in range(1, 4):
        total += jnp.dot(blocks[k][...], facing_ref[k], preferred_element_type=jnp.float32)
    send_ref[...] = total.astype(send_ref.dtype)
    for fetch in fetches:
        fetch.wait()
    total = jnp.dot(blocks[0][...], weight_buf[0], preferred_element_type=jnp.float32)
    for k in range(1, 4):
        total += jnp.dot(blocks[k][...], weight_buf[k], preferred_element_type=jnp.float32)
    own_ref[...] = total


def project(blocks, facing, weight, place, after):
    rows, depth = blocks[0].shape
    width = weight.shape[2]
    return pl.pallas_call(
        project_kernel,
        in_specs=[IN_SMEM] + [IN_VMEM] * 5 + [IN_HBM] + [IN_PLACE] * len(after),
        out_specs=[IN_VMEM] * 2,
        out_shape=[
            jax.ShapeDtypeStruct((rows, width), jnp.bfloat16),
            jax.ShapeDtypeStruct((rows, width), jnp.float32),
        ],
        scratch_shapes=[
            pltpu.VMEM((4, depth, width), weight.dtype),
            pltpu.SemaphoreType.DMA((4,)),
        ],
        compiler_params=params(),
        cost_estimate=cost(PROJECT_US),
        name="project",
    )(place, *blocks, facing, in_hbm(weight), *after)


def finish_kernel(own_ref, other_ref, *refs):
    out_ref = refs[-1]
    total = own_ref[...] + other_ref[...].astype(jnp.float32)
    out_ref[...] = total.astype(out_ref.dtype).reshape(out_ref.shape)


def finish(own, other, out, offset, steps_all, after):
    rows, width = own.shape
    steps = rows // SEGS
    in_specs = [IN_VMEM] * 2 + [IN_PLACE] * len(after)
    args = [own, other, *after]
    aliases = {}
    if out is not None:
        in_specs.append(IN_HBM)
        args.append(out)
        aliases = {len(args) - 1: 0}
    return pl.pallas_call(
        finish_kernel,
        grid=(1,),
        in_specs=in_specs,
        out_specs=pl.BlockSpec((SEGS, steps, width), lambda n: (0, offset // steps, 0)),
        out_shape=jax.ShapeDtypeStruct((SEGS, steps_all, width), jnp.bfloat16),
        input_output_aliases=aliases,
        compiler_params=params(),
        cost_estimate=cost(FINISH_US),
        name="finish",
    )(*args)


def hold_kernel(*refs):
    pass


def hold(value, after):
    return pl.pallas_call(
        hold_kernel,
        in_specs=[IN_VMEM] + [IN_PLACE] * len(after),
        out_specs=IN_VMEM,
        out_shape=jax.ShapeDtypeStruct(value.shape, value.dtype),
        input_output_aliases={0: 0},
        compiler_params=params(),
        cost_estimate=cost(0.3),
        name="hold",
    )(value, *after)


def to_chan(value, target):
    return lax.ppermute(value, "chan", [(i, target(i)) for i in range(8)])


def flip_chip(i):
    return i ^ 2


def flip_core(i):
    return i ^ 1


def facing_chip(i):
    return 2 * (3 - i // 2) + i % 2


def along_y(value, by):
    return lax.ppermute(
        value, "seq", [(s, s // 4 * 4 + (s % 4 + by) % 4) for s in range(16)]
    )


def along_z(value, by):
    return lax.ppermute(value, "seq", [(s, s + 4 * by) for s in range(16) if s + 4 * by < 16])


def around_z(value):
    return lax.ppermute(value, "seq", [(s, (s + 4) % 16) for s in range(16)])


def row_kernel(place_ref, rate_ref, *refs):
    near, (total_ref, ahead_ref) = refs[:4], refs[-2:]
    y = place_ref[0]
    step = rate_ref[...] * place_ref[1].astype(jnp.float32)
    total = jnp.zeros_like(step)
    ahead = jnp.zeros_like(step)
    for by in range(4):
        source = jnp.where(y >= by, y - by, y - by + 4)
        value = near[by][...]
        total = total + jnp.exp(-step * (3 - source).astype(jnp.float32)) * value
        if by:
            ahead = ahead + jnp.where(y >= by, jnp.exp(-step * (by - 1.0)) * value, 0.0)
    total_ref[...] = total
    ahead_ref[...] = ahead


def column_kernel(place_ref, rate_ref, ahead_ref, *refs):
    far, out_ref = refs[:3], refs[-1]
    step = rate_ref[...] * place_ref[1].astype(jnp.float32)
    total = far[0][...]
    for by in (1, 2):
        total = total + jnp.exp(-step * (4.0 * by)) * far[by][...]
    decay = jnp.exp(-step * place_ref[0].astype(jnp.float32))
    out_ref[...] = ahead_ref[...] + decay * total


def arriving_state(closing, rate, place, after):
    same = jax.ShapeDtypeStruct(closing.shape, closing.dtype)
    near = [closing] + [along_y(closing, by) for by in (1, 2, 3)]
    total, ahead = pl.pallas_call(
        row_kernel,
        in_specs=[IN_SMEM] + [IN_VMEM] * 5 + [IN_PLACE] * len(after),
        out_specs=[IN_VMEM] * 2,
        out_shape=[same, same],
        compiler_params=params(),
        name="row_state",
    )(place, rate, *near, *after)
    return pl.pallas_call(
        column_kernel,
        in_specs=[IN_SMEM] + [IN_VMEM] * 5,
        out_specs=IN_VMEM,
        out_shape=same,
        compiler_params=params(),
        name="column_state",
    )(place, rate, ahead, *[along_z(total, by) for by in (1, 2, 3)])


PARTS = (48, 48, 48, 48)
PROJECT_US = 0.1
FINISH_US = 1.0


def shards(gate_query, key_proj, value_proj, decay_rates, residues, skip_weight, out_weight):
    rows_here, width_here = key_proj.shape
    steps_all = rows_here // SEGS
    chan = lax.axis_index("chan")
    chip, core = chan // 2, chan % 2
    seq = lax.axis_index("seq")
    y = seq % 4
    quarter_at = (y + 2 * (seq // 4)) % 4

    def wanted(chip, core):
        return [
            2 * chip + core,
            2 * (chip ^ 1) + core,
            2 * chip + (1 - core),
            2 * (chip ^ 1) + (1 - core),
        ]

    weight = out_weight.reshape(8, width_here, width_here)
    facing = jnp.stack(wanted(3 - chip, core))
    place = jnp.concatenate(
        [jnp.stack([y, rows_here]), (quarter_at - jnp.arange(4)) % 4, jnp.stack(wanted(chip, core))]
    ).astype(jnp.int32)
    own_quarter = lax.dynamic_index_in_dim(weight, facing[quarter_at], 0, keepdims=False)
    quarter = to_chan(own_quarter, facing_chip)

    p, entry, closing = closing_pass(key_proj, value_proj, decay_rates)
    arriving = arriving_state(closing, decay_rates, place, [quarter])
    gain = residues * jnp.sqrt(-jnp.expm1(-2.0 * decay_rates))

    facing_weight = stack_blocks(place, [quarter, along_y(quarter, 1), around_z(quarter), along_y(quarter, 3)])

    starts = [sum(PARTS[:part]) for part in range(len(PARTS))]
    count = len(PARTS)
    state = entry
    gates, nears, sides, sends, owns, others = [], [], [], [], [], []

    def open_part(part):
        nonlocal state
        after = [nears[part - 2]] if part >= 2 else []
        if part == 1:
            after.append(sides[0])
        if part == 2:
            after.append(facing_weight)
        if part >= 3:
            after.append(sends[part - 3])
        gated, state = gate_pass(
            p, gate_query, decay_rates, gain, skip_weight, state,
            arriving if part == 0 else None, starts[part], PARTS[part], after,
        )
        gates.append(gated.reshape(SEGS * PARTS[part], width_here))
        nears.append(to_chan(gates[part], flip_chip))
        sides.append(to_chan(gates[part], flip_core))

    open_part(0)
    open_part(1)
    for part in range(count):
        if part + 2 < count:
            open_part(part + 2)
        if part >= 2:
            nears[part] = hold(nears[part], [others[part - 2], sends[part - 1]])
        blocks = [gates[part], nears[part], sides[part], to_chan(nears[part], flip_core)]
        after = [gates[part + 2]] if part + 2 < count else []
        send, own = project(blocks, facing_weight, weight, place, after)
        sends.append(send)
        owns.append(own)
        others.append(to_chan(send, facing_chip))
    out = None
    for part in range(count):
        after = [sends[part + 1]] if part + 1 < count else []
        out = finish(owns[part], others[part], out, starts[part], steps_all, after)
    return out.reshape(rows_here, width_here)


def solution(mesh):
    in_specs = (
        P("seq", "chan"),
        P("seq", "chan"),
        P("seq", "chan"),
        P(None, "chan"),
        P(None, "chan"),
        P("chan"),
        P(None, "chan"),
    )
    out_specs = P("seq", "chan")
    return jax.shard_map(shards, mesh=mesh, in_specs=in_specs, out_specs=out_specs, check_vma=False)
```

```python
import functools

import jax
import jax.numpy as jnp
from jax import lax
from jax.experimental import pallas as pl
from jax.experimental.pallas import tpu as pltpu
from jax.sharding import PartitionSpec as P

SEGS = 8
ROLE_SEGS = 4
LANES = 128
LOADS = 4
IN_VMEM = pl.BlockSpec(memory_space=pltpu.VMEM)
IN_SMEM = pl.BlockSpec(memory_space=pltpu.SMEM)
IN_PLACE = pl.BlockSpec(memory_space=pl.ANY)
IN_HBM = pl.BlockSpec(memory_space=pltpu.HBM)


def params(mebibytes=8):
    return pltpu.CompilerParams(vmem_limit_bytes=mebibytes << 20)


def in_hbm(value):
    return pltpu.with_memory_space_constraint(value, pltpu.HBM)


def position():
    seq, chan = lax.axis_index("seq"), lax.axis_index("chan")
    return lax.div(seq, 4), lax.rem(seq, 4), lax.div(chan, 2), lax.rem(chan, 2)


def mate_chip(chip, core):
    return jnp.where(core == 0, jnp.bitwise_xor(chip, 1), 3 - chip)


def face_chip(chip, core):
    return jnp.where(core == 0, 3 - chip, jnp.bitwise_xor(chip, 1))


def depth_block(chip, core, k):
    at_chip = jnp.where(k % 2 == 1, mate_chip(chip, core), chip)
    return 2 * at_chip + jnp.bitwise_xor(core, k // 2)


def own_quarter():
    z, y, chip, core = position()
    return lax.rem(y + 2 * z, 4)


def cost(microseconds):
    return pl.CostEstimate(flops=int(microseconds * 1.15e9), bytes_accessed=0, transcendentals=0)


def spread(row):
    return jnp.broadcast_to(row, (SEGS, LANES))


def tiles(width):
    return [slice(at, at + LANES) for at in range(0, width, LANES)]


def closing_kernel(
    k_hbm, v_hbm, rate_hbm, weight_hbm, quarter_hbm, p_ref, entry_ref, closing_ref, rate_ref,
    sibling_ref, k_buf, v_buf, flat_ref, state_ref, sems, other_sems,
):
    modes, width = rate_ref.shape
    steps = p_ref.shape[0]
    span = steps // LOADS
    stride = span + 1
    rate_copy = pltpu.make_async_copy(rate_hbm, rate_ref, other_sems.at[0])
    rate_copy.start()
    copies = []
    for i in range(LOADS):
        here = pl.ds(i * span, span)
        pair = [
            pltpu.make_async_copy(src.at[:, here, :], buf.at[i], sems.at[which, i])
            for which, (src, buf) in enumerate(((k_hbm, k_buf), (v_hbm, v_buf)))
        ]
        for copy in pair:
            copy.start()
        copies.append(pair)
    z, y, chip, core = position()
    weight_copies = [
        pltpu.make_async_copy(
            weight_hbm.at[depth_block(chip, 1 - core, k)], sibling_ref.at[k], other_sems.at[1 + k]
        )
        for k in range(4)
    ]
    for copy in weight_copies:
        copy.start()
    rate_copy.wait()
    rate = rate_ref[...]
    pole = jnp.exp(-rate)
    for i in range(LOADS):
        for copy in copies[i]:
            copy.wait()
        for cols in tiles(width):
            for s in range(SEGS):
                flat_ref[s * stride : s * stride + span, :] = k_buf[i, s, :, cols].astype(
                    jnp.float32
                ) * v_buf[i, s, :, cols].astype(jnp.float32)
            poles = [spread(pole[m : m + 1, cols]) for m in range(modes)]

            def step(t, states):
                x = flat_ref[pl.ds(t, SEGS, stride=stride), :]
                p_ref[i * span + t, :, cols] = x
                return tuple(a * s + x for a, s in zip(poles, states))

            if i == 0:
                states = (jnp.zeros((SEGS, LANES), jnp.float32),) * modes
            else:
                states = tuple(state_ref[m, :, cols] for m in range(modes))
            states = lax.fori_loop(0, span, step, states, unroll=UNROLL_CLOSING)
            for m in range(modes):
                state_ref[m, :, cols] = states[m]
    once = jnp.exp(-rate * steps)
    twice = once * once
    hops = ((1, once), (2, twice), (4, twice * twice))
    segment = lax.broadcasted_iota(jnp.int32, (SEGS, LANES), 0)
    for cols in tiles(width):
        for m in range(modes):
            total = state_ref[m, :, cols]
            for hop, decay in hops:
                moved = jnp.where(segment >= hop, pltpu.roll(total, hop, 0), 0.0)
                total = total + spread(decay[m : m + 1, cols]) * moved
            entry_ref[m, :, cols] = jnp.where(segment >= 1, pltpu.roll(total, 1, 0), 0.0)
            closing_ref[m : m + 1, cols] = total[SEGS - 1 :, :]
    for copy in weight_copies:
        copy.wait()


UNROLL_CLOSING = 16
CLOSING_GRANT = 12
CLOSING_US = 2.3
PICK_US = 0.7
MERGE_US = 0.4
GATE_US = 1.65
UNROLL_GATE = 4


def quarter_kernel(weight_hbm, first_ref, second_ref, sems):
    z, y, chip, core = position()
    k = own_quarter()
    copies = []
    for i, out_ref in enumerate((first_ref, second_ref)):
        target = jnp.bitwise_xor(core, i)
        target_chip = face_chip(chip, target)
        at_chip = jnp.where(lax.rem(k, 2) == 1, mate_chip(target_chip, target), target_chip)
        block = 2 * at_chip + jnp.bitwise_xor(target, lax.div(k, 2))
        copies.append(pltpu.make_async_copy(weight_hbm.at[block], out_ref, sems.at[i]))
        copies[i].start()
    for copy in copies:
        copy.wait()


def pick_quarters(weight):
    return pl.pallas_call(
        quarter_kernel,
        in_specs=[IN_HBM],
        out_specs=[IN_VMEM] * 2,
        out_shape=[jax.ShapeDtypeStruct(weight.shape[1:], weight.dtype)] * 2,
        scratch_shapes=[pltpu.SemaphoreType.DMA((2,))],
        compiler_params=params(),
        cost_estimate=cost(PICK_US),
        name="pick_quarters",
    )(in_hbm(weight))


def merge_kernel(first_ref, second_ref, *refs):
    out_ref = refs[-1]
    width = first_ref.shape[1]
    out_ref[:, :width] = first_ref[...]
    out_ref[:, width:] = second_ref[...]


def merge(first, second, after):
    return pl.pallas_call(
        merge_kernel,
        in_specs=[IN_VMEM] * 2 + [IN_PLACE] * len(after),
        out_specs=IN_VMEM,
        out_shape=jax.ShapeDtypeStruct((first.shape[0], 2 * first.shape[1]), first.dtype),
        compiler_params=params(),
        cost_estimate=cost(MERGE_US),
        name="merge",
    )(first, second, *after)


def closing_pass(k, v, rate, weight, quarter):
    rows, width = k.shape
    modes = rate.shape[0]
    steps = rows // SEGS
    span = steps // LOADS
    buffer = pltpu.VMEM((LOADS, SEGS, span, width), k.dtype)
    return pl.pallas_call(
        closing_kernel,
        in_specs=[IN_HBM] * 4 + [IN_PLACE],
        out_specs=[IN_VMEM] * 5,
        out_shape=[
            jax.ShapeDtypeStruct((steps, SEGS, width), jnp.float32),
            jax.ShapeDtypeStruct((modes, SEGS, width), jnp.float32),
            jax.ShapeDtypeStruct((modes, width), jnp.float32),
            jax.ShapeDtypeStruct((modes, width), jnp.float32),
            jax.ShapeDtypeStruct((4,) + weight.shape[1:], weight.dtype),
        ],
        scratch_shapes=[
            buffer,
            buffer,
            pltpu.VMEM((SEGS * (span + 1), LANES), jnp.float32),
            pltpu.VMEM((modes, SEGS, width), jnp.float32),
            pltpu.SemaphoreType.DMA((2, LOADS)),
            pltpu.SemaphoreType.DMA((5,)),
        ],
        compiler_params=params(CLOSING_GRANT),
        cost_estimate=cost(CLOSING_US),
        name="closing_pass",
    )(
        in_hbm(k.reshape(SEGS, steps, width)),
        in_hbm(v.reshape(SEGS, steps, width)),
        in_hbm(rate),
        in_hbm(weight),
        quarter,
    )


def gate_kernel(first, waits, offset, p_ref, q_hbm, rate_ref, gain_ref, skip_ref, *rest):
    arriving_ref = rest[0]
    entry_ref = rest[int(first)]
    mine_ref, other_ref, after_ref, flat_ref, q_buf, sem = rest[int(first) + 1 + waits :]
    modes, width = rate_ref.shape
    steps = mine_ref.shape[0] // ROLE_SEGS
    stride = steps + 1
    fetch = pltpu.make_async_copy(q_hbm.at[:, pl.ds(offset, steps), :], q_buf, sem)
    fetch.start()
    rate = rate_ref[...]
    pole = jnp.exp(-rate)
    if first:
        once = jnp.exp(-rate * p_ref.shape[0])
        twice = once * once
        fourth = twice * twice
        segment = lax.broadcasted_iota(jnp.int32, (SEGS, LANES), 0)
        odd, upper, top = (segment % 2 >= 1, segment % 4 >= 2, segment >= 4)
    for at, cols in enumerate(tiles(width)):
        poles = [spread(pole[m : m + 1, cols]) for m in range(modes)]
        gains = [spread(gain_ref[m : m + 1, cols]) for m in range(modes)]
        skip = spread(skip_ref[:, cols])
        states = []
        for m in range(modes):
            state = entry_ref[m, :, cols]
            if first:
                carried = spread(arriving_ref[m : m + 1, cols])
                for picked, decay in ((odd, once), (upper, twice), (top, fourth)):
                    carried = jnp.where(picked, carried * spread(decay[m : m + 1, cols]), carried)
                state = state + carried
            states.append(state)

        def step(t, states):
            x = p_ref[offset + t, :, cols]
            states = tuple(a * s + x for a, s in zip(poles, states))
            terms = [g * s for g, s in zip(gains, states)] + [skip * x]
            while len(terms) > 1:
                terms = [
                    terms[i] + terms[i + 1] if i + 1 < len(terms) else terms[i]
                    for i in range(0, len(terms), 2)
                ]
            flat_ref[at, pl.ds(t, SEGS, stride=stride), :] = terms[0]
            return states

        states = lax.fori_loop(0, steps, step, tuple(states), unroll=UNROLL_GATE)
        for m in range(modes):
            after_ref[m, :, cols] = states[m]
    fetch.wait()
    z, y, chip, core = position()
    for mine in (0, 1):

        @pl.when(core == mine)
        def _():
            for at, cols in enumerate(tiles(width)):
                for s in range(SEGS):
                    y = flat_ref[at, s * stride : s * stride + steps, :]
                    q = q_buf[s, :, cols].astype(jnp.float32)
                    target = mine_ref if s // ROLE_SEGS == mine else other_ref
                    rows = slice(s % ROLE_SEGS * steps, (s % ROLE_SEGS + 1) * steps)
                    target[rows, cols] = (q * y).astype(jnp.bfloat16)


def gate_pass(p, q, rate, gain, skip, entry, arriving, offset, steps, after):
    steps_all, segs, width = p.shape
    modes = rate.shape[0]
    first = arriving is not None
    args = [p, in_hbm(q.reshape(SEGS, steps_all, width)), rate, gain, skip.reshape(1, width)]
    args += ([arriving] if first else []) + [entry]
    in_specs = [IN_VMEM] * len(args) + [IN_PLACE] * len(after)
    in_specs[1] = IN_HBM
    return pl.pallas_call(
        functools.partial(gate_kernel, first, len(after), offset),
        in_specs=in_specs,
        out_specs=[IN_VMEM] * 3,
        out_shape=[
            jax.ShapeDtypeStruct((ROLE_SEGS * steps, width), jnp.bfloat16),
            jax.ShapeDtypeStruct((ROLE_SEGS * steps, width), jnp.bfloat16),
            jax.ShapeDtypeStruct((modes, SEGS, width), jnp.float32),
        ],
        scratch_shapes=[
            pltpu.VMEM((width // LANES, SEGS * (steps + 1), LANES), jnp.float32),
            pltpu.VMEM((SEGS, steps, width), q.dtype),
            pltpu.SemaphoreType.DMA,
        ],
        compiler_params=params(),
        cost_estimate=cost(GATE_US * steps / 96),
        name="gate_pass",
    )(*args, *after)


def stack_kernel(*refs):
    pieces, out_ref = refs[:4], refs[-1]
    k = own_quarter()
    for i, piece in enumerate(pieces):
        out_ref[lax.rem(k + 4 - i, 4)] = piece[...]


def stack_blocks(pieces, after):
    return pl.pallas_call(
        stack_kernel,
        in_specs=[IN_VMEM] * len(pieces) + [IN_PLACE] * len(after),
        out_specs=IN_VMEM,
        out_shape=jax.ShapeDtypeStruct((len(pieces),) + pieces[0].shape, pieces[0].dtype),
        compiler_params=params(),
        cost_estimate=cost(STACK_US),
        name="stack_blocks",
    )(*pieces, *after)


def send_kernel(*refs):
    blocks, facing_ref, (first_ref, second_ref) = refs[:4], refs[4], refs[-2:]
    width = first_ref.shape[1]
    total = jnp.dot(blocks[0][...], facing_ref[0], preferred_element_type=jnp.float32)
    for k in range(1, 4):
        total += jnp.dot(blocks[k][...], facing_ref[k], preferred_element_type=jnp.float32)
    first_ref[...] = total[:, :width].astype(first_ref.dtype)
    second_ref[...] = total[:, width:].astype(second_ref.dtype)


def send_products(blocks, facing, after):
    rows = blocks[0].shape[0]
    width = facing.shape[2] // 2
    return pl.pallas_call(
        send_kernel,
        in_specs=[IN_VMEM] * 5 + [IN_PLACE] * len(after),
        out_specs=[IN_VMEM] * 2,
        out_shape=[jax.ShapeDtypeStruct((rows, width), jnp.bfloat16)] * 2,
        compiler_params=params(),
        cost_estimate=cost(SEND_US),
        name="send_products",
    )(*blocks, facing, *after)


def side_kernel(*refs):
    blocks, sibling_ref, out_ref = refs[:4], refs[4], refs[-1]
    total = jnp.dot(blocks[0][...], sibling_ref[0], preferred_element_type=jnp.float32)
    for k in range(1, 4):
        total += jnp.dot(blocks[k][...], sibling_ref[k], preferred_element_type=jnp.float32)
    out_ref[...] = total


def side_products(blocks, sibling, after):
    rows = blocks[0].shape[0]
    width = sibling.shape[2]
    return pl.pallas_call(
        side_kernel,
        in_specs=[IN_VMEM] * 5 + [IN_PLACE] * len(after),
        out_specs=IN_VMEM,
        out_shape=jax.ShapeDtypeStruct((rows, width), jnp.float32),
        compiler_params=params(),
        cost_estimate=cost(SIDE_US),
        name="side_products",
    )(*blocks, sibling, *after)


def own_kernel(*refs):
    blocks, weight_hbm = refs[:4], refs[4]
    out_ref, weight_buf, sems = refs[-3:]
    z, y, chip, core = position()
    fetches = [
        pltpu.make_async_copy(
            weight_hbm.at[depth_block(chip, core, k)], weight_buf.at[k], sems.at[k]
        )
        for k in range(4)
    ]
    for fetch in fetches:
        fetch.start()
    fetches[0].wait()
    total = jnp.dot(blocks[0][...], weight_buf[0], preferred_element_type=jnp.float32)
    for k in range(1, 4):
        fetches[k].wait()
        total += jnp.dot(blocks[k][...], weight_buf[k], preferred_element_type=jnp.float32)
    out_ref[...] = total


def own_products(blocks, weight, after):
    rows, depth = blocks[0].shape
    width = weight.shape[2]
    return pl.pallas_call(
        own_kernel,
        in_specs=[IN_VMEM] * 4 + [IN_HBM] + [IN_PLACE] * len(after),
        out_specs=IN_VMEM,
        out_shape=jax.ShapeDtypeStruct((rows, width), jnp.float32),
        scratch_shapes=[
            pltpu.VMEM((4, depth, width), weight.dtype),
            pltpu.SemaphoreType.DMA((4,)),
        ],
        compiler_params=params(),
        cost_estimate=cost(OWN_US),
        name="own_products",
    )(*blocks, in_hbm(weight), *after)


def finish_kernel(offset, own_ref, first_ref, side_ref, second_ref, *refs):
    out_hbm, block_ref, sem = refs[-3:]
    z, y, chip, core = position()
    shape = (ROLE_SEGS,) + block_ref.shape[1:]
    mine = (own_ref[...] + first_ref[...].astype(jnp.float32)).astype(block_ref.dtype)
    other = (side_ref[...] + second_ref[...].astype(jnp.float32)).astype(block_ref.dtype)
    block_ref[pl.ds(core * ROLE_SEGS, ROLE_SEGS)] = mine.reshape(shape)
    block_ref[pl.ds((1 - core) * ROLE_SEGS, ROLE_SEGS)] = other.reshape(shape)
    here = pl.ds(offset, block_ref.shape[1])
    copy = pltpu.make_async_copy(block_ref, out_hbm.at[:, here, :], sem)
    copy.start()
    copy.wait()


def finish(own, first, side, second, out, offset, steps_all, after):
    rows, width = own.shape
    steps = rows // ROLE_SEGS
    in_specs = [IN_VMEM] * 4 + [IN_PLACE] * len(after)
    args = [own, first, side, second, *after]
    aliases = {}
    if out is not None:
        in_specs.append(IN_HBM)
        args.append(out)
        aliases = {len(args) - 1: 0}
    return pl.pallas_call(
        functools.partial(finish_kernel, offset),
        in_specs=in_specs,
        out_specs=IN_HBM,
        out_shape=jax.ShapeDtypeStruct((SEGS, steps_all, width), jnp.bfloat16),
        scratch_shapes=[
            pltpu.VMEM((SEGS, steps, width), jnp.bfloat16),
            pltpu.SemaphoreType.DMA,
        ],
        input_output_aliases=aliases,
        compiler_params=params(),
        cost_estimate=cost(FINISH_US),
        name="finish",
    )(*args)


def to_chan(value, target):
    return lax.ppermute(value, "chan", [(i, target(i)) for i in range(8)])


def flip_core(i):
    return i ^ 1


def mate(i):
    return i ^ 2 if i % 2 == 0 else 2 * (3 - i // 2) + 1


def face(i):
    return 2 * (3 - i // 2) if i % 2 == 0 else i ^ 2


def mate_across(i):
    return mate(i ^ 1)


def face_across(i):
    return face(i) ^ 1


def face_other_role(i):
    return face(i ^ 1)


def along_y(value, by):
    return lax.ppermute(
        value, "seq", [(s, s // 4 * 4 + (s % 4 + by) % 4) for s in range(16)]
    )


def along_z(value, by):
    return lax.ppermute(value, "seq", [(s, s + 4 * by) for s in range(16) if s + 4 * by < 16])


def around_z(value):
    return lax.ppermute(value, "seq", [(s, (s + 4) % 16) for s in range(16)])


def row_kernel(block_rows, rate_ref, *refs):
    near, (total_ref, ahead_ref) = refs[:4], refs[-2:]
    z, y, chip, core = position()
    step = rate_ref[...] * float(block_rows)
    total = jnp.zeros_like(step)
    ahead = jnp.zeros_like(step)
    for by in range(4):
        source = jnp.where(y >= by, y - by, y - by + 4)
        value = near[by][...]
        total = total + jnp.exp(-step * (3 - source).astype(jnp.float32)) * value
        if by:
            ahead = ahead + jnp.where(y >= by, jnp.exp(-step * (by - 1.0)) * value, 0.0)
    total_ref[...] = total
    ahead_ref[...] = ahead


def column_kernel(block_rows, rate_ref, ahead_ref, *refs):
    far, out_ref = refs[:3], refs[-1]
    z, y, chip, core = position()
    step = rate_ref[...] * float(block_rows)
    total = far[0][...]
    for by in (1, 2):
        total = total + jnp.exp(-step * (4.0 * by)) * far[by][...]
    decay = jnp.exp(-step * y.astype(jnp.float32))
    out_ref[...] = ahead_ref[...] + decay * total


def arriving_state(closing, rate, block_rows):
    same = jax.ShapeDtypeStruct(closing.shape, closing.dtype)
    near = [closing] + [along_y(closing, by) for by in (1, 2, 3)]
    total, ahead = pl.pallas_call(
        functools.partial(row_kernel, block_rows),
        in_specs=[IN_VMEM] * 5,
        out_specs=[IN_VMEM] * 2,
        out_shape=[same, same],
        compiler_params=params(),
        cost_estimate=cost(ROW_US),
        name="row_state",
    )(rate, *near)
    arriving = pl.pallas_call(
        functools.partial(column_kernel, block_rows),
        in_specs=[IN_VMEM] * 5,
        out_specs=IN_VMEM,
        out_shape=same,
        compiler_params=params(),
        cost_estimate=cost(COLUMN_US),
        name="column_state",
    )(rate, ahead, *[along_z(total, by) for by in (1, 2, 3)])
    return arriving, total


PARTS = (96, 96)
SEND_US = 1.4
SIDE_US = 0.8
STACK_US = 0.5
ROW_US = 2.0
COLUMN_US = 2.0
DEPS = 'RK'
FINISH_US = 0.3
OWN_US = 0.8


def shards(gate_query, key_proj, value_proj, decay_rates, residues, skip_weight, out_weight):
    rows_here, width_here = key_proj.shape
    steps_all = rows_here // SEGS
    weight = out_weight.reshape(8, width_here, width_here)
    quarters = pick_quarters(weight)
    first_quarter = to_chan(quarters[0], face)
    second_quarter = to_chan(quarters[1], face_other_role)
    p, entry, closing, rate, for_sibling = closing_pass(
        key_proj, value_proj, decay_rates, weight, quarters[0]
    )
    arriving, total = arriving_state(closing, rate, rows_here)
    quarter = merge(first_quarter, second_quarter, [total] if "R" in DEPS else [])
    pieces = [quarter, along_y(quarter, 1), around_z(quarter), along_y(quarter, 3)]
    gain = residues * jnp.sqrt(-jnp.expm1(-2.0 * decay_rates))

    starts = [sum(PARTS[:part]) for part in range(len(PARTS))]
    count = len(PARTS)
    state = entry
    blocks = []
    for part, steps in enumerate(PARTS):
        mine, other, state = gate_pass(
            p, gate_query, rate, gain, skip_weight, state,
            arriving if part == 0 else None, starts[part], steps, [],
        )
        blocks.append(
            [mine, to_chan(mine, mate), to_chan(other, flip_core), to_chan(other, mate_across)]
        )
    sibling = to_chan(for_sibling, flip_core)
    firsts, seconds, sides = [], [], []
    facing = None
    after = []
    for part in range(count):
        side = side_products(blocks[part], sibling, after)
        sides.append(to_chan(side, flip_core))
        if facing is None:
            facing = stack_blocks(pieces, [side] if "T" in DEPS else [])
        first, second = send_products(blocks[part], facing, [side] if "V" in DEPS else [])
        firsts.append(to_chan(first, face))
        seconds.append(to_chan(second, face_across))
        after = [first] if "W" in DEPS else []
    out = None
    owns = [own_products(blocks[part], weight, [first] if "K" in DEPS else []) for part in range(count)]
    for part in range(count):
        out = finish(
            owns[part], firsts[part], sides[part], seconds[part], out, starts[part], steps_all, []
        )
    return out.reshape(rows_here, width_here)


def solution(mesh):
    in_specs = (
        P("seq", "chan"),
        P("seq", "chan"),
        P("seq", "chan"),
        P(None, "chan"),
        P(None, "chan"),
        P("chan"),
        P(None, "chan"),
    )
    out_specs = P("seq", "chan")
    return jax.shard_map(shards, mesh=mesh, in_specs=in_specs, out_specs=out_specs, check_vma=False)
```

```python
import functools

import jax
import jax.numpy as jnp
from jax import lax
from jax.experimental import pallas as pl
from jax.experimental.pallas import tpu as pltpu
from jax.sharding import PartitionSpec as P

SEGS = 8
ROLE_SEGS = 4
LANES = 128
LOADS = 4
IN_VMEM = pl.BlockSpec(memory_space=pltpu.VMEM)
IN_SMEM = pl.BlockSpec(memory_space=pltpu.SMEM)
IN_PLACE = pl.BlockSpec(memory_space=pl.ANY)
IN_HBM = pl.BlockSpec(memory_space=pltpu.HBM)


def params(mebibytes=8):
    return pltpu.CompilerParams(vmem_limit_bytes=mebibytes << 20)


def in_hbm(value):
    return pltpu.with_memory_space_constraint(value, pltpu.HBM)


def position():
    seq, chan = lax.axis_index("seq"), lax.axis_index("chan")
    return lax.div(seq, 4), lax.rem(seq, 4), lax.div(chan, 2), lax.rem(chan, 2)


def mate_chip(chip, core):
    return jnp.where(core == 0, jnp.bitwise_xor(chip, 1), 3 - chip)


def face_chip(chip, core):
    return jnp.where(core == 0, 3 - chip, jnp.bitwise_xor(chip, 1))


def depth_block(chip, core, k):
    at_chip = jnp.where(k % 2 == 1, mate_chip(chip, core), chip)
    return 2 * at_chip + jnp.bitwise_xor(core, k // 2)


def own_quarter():
    z, y, chip, core = position()
    return lax.rem(y + 2 * z, 4)


def cost(microseconds):
    return pl.CostEstimate(flops=int(microseconds * 1.15e9), bytes_accessed=0, transcendentals=0)


def spread(row):
    return jnp.broadcast_to(row, (SEGS, LANES))


def tiles(width):
    return [slice(at, at + LANES) for at in range(0, width, LANES)]


def closing_kernel(
    k_hbm, v_hbm, rate_hbm, weight_hbm, quarter_hbm, p_ref, entry_ref, closing_ref, rate_ref,
    sib0_ref, sib1_ref, sib2_ref, sib3_ref, k_buf, v_buf, flat_ref, state_ref, sems, other_sems,
):
    modes, width = rate_ref.shape
    steps = p_ref.shape[0]
    span = steps // LOADS
    stride = span + 1
    rate_copy = pltpu.make_async_copy(rate_hbm, rate_ref, other_sems.at[0])
    rate_copy.start()
    copies = []
    for i in range(LOADS):
        here = pl.ds(i * span, span)
        pair = [
            pltpu.make_async_copy(src.at[:, here, :], buf.at[i], sems.at[which, i])
            for which, (src, buf) in enumerate(((k_hbm, k_buf), (v_hbm, v_buf)))
        ]
        for copy in pair:
            copy.start()
        copies.append(pair)
    z, y, chip, core = position()
    weight_copies = [
        pltpu.make_async_copy(
            weight_hbm.at[depth_block(chip, 1 - core, k)], out_ref, other_sems.at[1 + k]
        )
        for k, out_ref in enumerate((sib0_ref, sib1_ref, sib2_ref, sib3_ref))
    ]
    for copy in weight_copies:
        copy.start()
    rate_copy.wait()
    rate = rate_ref[...]
    pole = jnp.exp(-rate)
    for i in range(LOADS):
        for copy in copies[i]:
            copy.wait()
        for cols in tiles(width):
            for s in range(SEGS):
                flat_ref[s * stride : s * stride + span, :] = k_buf[i, s, :, cols].astype(
                    jnp.float32
                ) * v_buf[i, s, :, cols].astype(jnp.float32)
            poles = [spread(pole[m : m + 1, cols]) for m in range(modes)]

            def step(t, states):
                x = flat_ref[pl.ds(t, SEGS, stride=stride), :]
                p_ref[i * span + t, :, cols] = x
                return tuple(a * s + x for a, s in zip(poles, states))

            if i == 0:
                states = (jnp.zeros((SEGS, LANES), jnp.float32),) * modes
            else:
                states = tuple(state_ref[m, :, cols] for m in range(modes))
            states = lax.fori_loop(0, span, step, states, unroll=UNROLL_CLOSING)
            for m in range(modes):
                state_ref[m, :, cols] = states[m]
    once = jnp.exp(-rate * steps)
    twice = once * once
    hops = ((1, once), (2, twice), (4, twice * twice))
    segment = lax.broadcasted_iota(jnp.int32, (SEGS, LANES), 0)
    for cols in tiles(width):
        for m in range(modes):
            total = state_ref[m, :, cols]
            for hop, decay in hops:
                moved = jnp.where(segment >= hop, pltpu.roll(total, hop, 0), 0.0)
                total = total + spread(decay[m : m + 1, cols]) * moved
            entry_ref[m, :, cols] = jnp.where(segment >= 1, pltpu.roll(total, 1, 0), 0.0)
            closing_ref[m : m + 1, cols] = total[SEGS - 1 :, :]
    for copy in weight_copies:
        copy.wait()


UNROLL_CLOSING = 16
CLOSING_GRANT = 12
CLOSING_US = 5.0
PICK_US = 0.7
MERGE_US = 0.4
GATE_US = 0.8
UNROLL_GATE = 16


def quarter_kernel(weight_hbm, first_ref, second_ref, sems):
    z, y, chip, core = position()
    k = own_quarter()
    copies = []
    for i, out_ref in enumerate((first_ref, second_ref)):
        target = jnp.bitwise_xor(core, i)
        target_chip = face_chip(chip, target)
        at_chip = jnp.where(lax.rem(k, 2) == 1, mate_chip(target_chip, target), target_chip)
        block = 2 * at_chip + jnp.bitwise_xor(target, lax.div(k, 2))
        copies.append(pltpu.make_async_copy(weight_hbm.at[block], out_ref, sems.at[i]))
        copies[i].start()
    for copy in copies:
        copy.wait()


def pick_quarters(weight):
    return pl.pallas_call(
        quarter_kernel,
        in_specs=[IN_HBM],
        out_specs=[IN_VMEM] * 2,
        out_shape=[jax.ShapeDtypeStruct(weight.shape[1:], weight.dtype)] * 2,
        scratch_shapes=[pltpu.SemaphoreType.DMA((2,))],
        compiler_params=params(),
        cost_estimate=cost(PICK_US),
        name="pick_quarters",
    )(in_hbm(weight))


def merge_kernel(first_ref, second_ref, *refs):
    out_ref = refs[-1]
    width = first_ref.shape[1]
    out_ref[:, :width] = first_ref[...]
    out_ref[:, width:] = second_ref[...]


def merge(first, second, after):
    return pl.pallas_call(
        merge_kernel,
        in_specs=[IN_VMEM] * 2 + [IN_PLACE] * len(after),
        out_specs=IN_VMEM,
        out_shape=jax.ShapeDtypeStruct((first.shape[0], 2 * first.shape[1]), first.dtype),
        compiler_params=params(),
        cost_estimate=cost(MERGE_US),
        name="merge",
    )(first, second, *after)


def closing_pass(k, v, rate, weight, quarter):
    rows, width = k.shape
    modes = rate.shape[0]
    steps = rows // SEGS
    span = steps // LOADS
    buffer = pltpu.VMEM((LOADS, SEGS, span, width), k.dtype)
    return pl.pallas_call(
        closing_kernel,
        in_specs=[IN_HBM] * 4 + [IN_PLACE],
        out_specs=[IN_VMEM] * 8,
        out_shape=[
            jax.ShapeDtypeStruct((steps, SEGS, width), jnp.float32),
            jax.ShapeDtypeStruct((modes, SEGS, width), jnp.float32),
            jax.ShapeDtypeStruct((modes, width), jnp.float32),
            jax.ShapeDtypeStruct((modes, width), jnp.float32),
        ]
        + [jax.ShapeDtypeStruct(weight.shape[1:], weight.dtype)] * 4,
        scratch_shapes=[
            buffer,
            buffer,
            pltpu.VMEM((SEGS * (span + 1), LANES), jnp.float32),
            pltpu.VMEM((modes, SEGS, width), jnp.float32),
            pltpu.SemaphoreType.DMA((2, LOADS)),
            pltpu.SemaphoreType.DMA((5,)),
        ],
        compiler_params=params(CLOSING_GRANT),
        cost_estimate=cost(CLOSING_US),
        name="closing_pass",
    )(
        in_hbm(k.reshape(SEGS, steps, width)),
        in_hbm(v.reshape(SEGS, steps, width)),
        in_hbm(rate),
        in_hbm(weight),
        quarter,
    )


def gate_kernel(first, waits, offset, p_ref, q_hbm, rate_ref, gain_ref, skip_ref, *rest):
    arriving_ref = rest[0]
    entry_ref = rest[int(first)]
    mine_ref, other_ref, after_ref, flat_ref, q_buf, sem = rest[int(first) + 1 + waits :]
    modes, width = rate_ref.shape
    steps = mine_ref.shape[0] // ROLE_SEGS
    stride = steps + 1
    fetch = pltpu.make_async_copy(q_hbm.at[:, pl.ds(offset, steps), :], q_buf, sem)
    fetch.start()
    rate = rate_ref[...]
    pole = jnp.exp(-rate)
    if first:
        once = jnp.exp(-rate * p_ref.shape[0])
        twice = once * once
        fourth = twice * twice
        segment = lax.broadcasted_iota(jnp.int32, (SEGS, LANES), 0)
        odd, upper, top = (segment % 2 >= 1, segment % 4 >= 2, segment >= 4)
    for at, cols in enumerate(tiles(width)):
        poles = [spread(pole[m : m + 1, cols]) for m in range(modes)]
        gains = [spread(gain_ref[m : m + 1, cols]) for m in range(modes)]
        skip = spread(skip_ref[:, cols])
        states = []
        for m in range(modes):
            state = entry_ref[m, :, cols]
            if first:
                carried = spread(arriving_ref[m : m + 1, cols])
                for picked, decay in ((odd, once), (upper, twice), (top, fourth)):
                    carried = jnp.where(picked, carried * spread(decay[m : m + 1, cols]), carried)
                state = state + carried
            states.append(state)

        def step(t, states):
            x = p_ref[offset + t, :, cols]
            states = tuple(a * s + x for a, s in zip(poles, states))
            terms = [g * s for g, s in zip(gains, states)] + [skip * x]
            while len(terms) > 1:
                terms = [
                    terms[i] + terms[i + 1] if i + 1 < len(terms) else terms[i]
                    for i in range(0, len(terms), 2)
                ]
            flat_ref[at, pl.ds(t, SEGS, stride=stride), :] = terms[0]
            return states

        states = lax.fori_loop(0, steps, step, tuple(states), unroll=UNROLL_GATE)
        for m in range(modes):
            after_ref[m, :, cols] = states[m]
    fetch.wait()
    z, y, chip, core = position()
    for mine in (0, 1):

        @pl.when(core == mine)
        def _():
            for at, cols in enumerate(tiles(width)):
                for s in range(SEGS):
                    y = flat_ref[at, s * stride : s * stride + steps, :]
                    q = q_buf[s, :, cols].astype(jnp.float32)
                    target = mine_ref if s // ROLE_SEGS == mine else other_ref
                    rows = slice(s % ROLE_SEGS * steps, (s % ROLE_SEGS + 1) * steps)
                    target[rows, cols] = (q * y).astype(jnp.bfloat16)


def gate_pass(p, q, rate, gain, skip, entry, arriving, offset, steps, after):
    steps_all, segs, width = p.shape
    modes = rate.shape[0]
    first = arriving is not None
    args = [p, in_hbm(q.reshape(SEGS, steps_all, width)), rate, gain, skip.reshape(1, width)]
    args += ([arriving] if first else []) + [entry]
    in_specs = [IN_VMEM] * len(args) + [IN_PLACE] * len(after)
    in_specs[1] = IN_HBM
    return pl.pallas_call(
        functools.partial(gate_kernel, first, len(after), offset),
        in_specs=in_specs,
        out_specs=[IN_VMEM] * 3,
        out_shape=[
            jax.ShapeDtypeStruct((ROLE_SEGS * steps, width), jnp.bfloat16),
            jax.ShapeDtypeStruct((ROLE_SEGS * steps, width), jnp.bfloat16),
            jax.ShapeDtypeStruct((modes, SEGS, width), jnp.float32),
        ],
        scratch_shapes=[
            pltpu.VMEM((width // LANES, SEGS * (steps + 1), LANES), jnp.float32),
            pltpu.VMEM((SEGS, steps, width), q.dtype),
            pltpu.SemaphoreType.DMA,
        ],
        compiler_params=params(),
        cost_estimate=cost(GATE_US * steps / 96),
        name="gate_pass",
    )(*args, *after)


def stack_kernel(*refs):
    pieces, out_ref = refs[:4], refs[-1]
    k = own_quarter()
    for i, piece in enumerate(pieces):
        out_ref[lax.rem(k + 4 - i, 4)] = piece[...]


def stack_blocks(pieces, after):
    return pl.pallas_call(
        stack_kernel,
        in_specs=[IN_VMEM] * len(pieces) + [IN_PLACE] * len(after),
        out_specs=IN_VMEM,
        out_shape=jax.ShapeDtypeStruct((len(pieces),) + pieces[0].shape, pieces[0].dtype),
        compiler_params=params(),
        cost_estimate=cost(STACK_US),
        name="stack_blocks",
    )(*pieces, *after)


def send_kernel(*refs):
    blocks, facing_ref, (first_ref, second_ref) = refs[:4], refs[4], refs[-2:]
    width = first_ref.shape[1]
    total = jnp.dot(blocks[0][...], facing_ref[0], preferred_element_type=jnp.float32)
    for k in range(1, 4):
        total += jnp.dot(blocks[k][...], facing_ref[k], preferred_element_type=jnp.float32)
    first_ref[...] = total[:, :width].astype(first_ref.dtype)
    second_ref[...] = total[:, width:].astype(second_ref.dtype)


def send_products(blocks, facing, after):
    rows = blocks[0].shape[0]
    width = facing.shape[2] // 2
    return pl.pallas_call(
        send_kernel,
        in_specs=[IN_VMEM] * 5 + [IN_PLACE] * len(after),
        out_specs=[IN_VMEM] * 2,
        out_shape=[jax.ShapeDtypeStruct((rows, width), jnp.bfloat16)] * 2,
        compiler_params=params(),
        cost_estimate=cost(SEND_US),
        name="send_products",
    )(*blocks, facing, *after)


def side_kernel(*refs):
    blocks, weights, out_ref = refs[:4], refs[4:8], refs[-1]
    total = jnp.dot(blocks[0][...], weights[0][...], preferred_element_type=jnp.float32)
    for k in range(1, 4):
        total += jnp.dot(blocks[k][...], weights[k][...], preferred_element_type=jnp.float32)
    out_ref[...] = total.astype(out_ref.dtype)


def side_products(blocks, sibling, after):
    rows = blocks[0].shape[0]
    width = sibling[0].shape[1]
    return pl.pallas_call(
        side_kernel,
        in_specs=[IN_VMEM] * 8 + [IN_PLACE] * len(after),
        out_specs=IN_VMEM,
        out_shape=jax.ShapeDtypeStruct((rows, width), jnp.bfloat16),
        compiler_params=params(),
        cost_estimate=cost(SIDE_US),
        name="side_products",
    )(*blocks, *sibling, *after)


def own_kernel(*refs):
    blocks, weight_hbm = refs[:4], refs[4]
    out_ref, weight_buf, sems = refs[-3:]
    z, y, chip, core = position()
    fetches = [
        pltpu.make_async_copy(
            weight_hbm.at[depth_block(chip, core, k)], weight_buf.at[k], sems.at[k]
        )
        for k in range(4)
    ]
    for fetch in fetches:
        fetch.start()
    fetches[0].wait()
    total = jnp.dot(blocks[0][...], weight_buf[0], preferred_element_type=jnp.float32)
    for k in range(1, 4):
        fetches[k].wait()
        total += jnp.dot(blocks[k][...], weight_buf[k], preferred_element_type=jnp.float32)
    out_ref[...] = total


def own_products(blocks, weight, after):
    rows, depth = blocks[0].shape
    width = weight.shape[2]
    return pl.pallas_call(
        own_kernel,
        in_specs=[IN_VMEM] * 4 + [IN_HBM] + [IN_PLACE] * len(after),
        out_specs=IN_VMEM,
        out_shape=jax.ShapeDtypeStruct((rows, width), jnp.float32),
        scratch_shapes=[
            pltpu.VMEM((4, depth, width), weight.dtype),
            pltpu.SemaphoreType.DMA((4,)),
        ],
        compiler_params=params(),
        cost_estimate=cost(OWN_US),
        name="own_products",
    )(*blocks, in_hbm(weight), *after)


def finish_kernel(offset, own_ref, first_ref, side_ref, second_ref, *refs):
    out_hbm, block_ref, sem = refs[-3:]
    z, y, chip, core = position()
    shape = (ROLE_SEGS,) + block_ref.shape[1:]
    mine = (own_ref[...] + first_ref[...].astype(jnp.float32)).astype(block_ref.dtype)
    other = (side_ref[...].astype(jnp.float32) + second_ref[...].astype(jnp.float32)).astype(block_ref.dtype)
    block_ref[pl.ds(core * ROLE_SEGS, ROLE_SEGS)] = mine.reshape(shape)
    block_ref[pl.ds((1 - core) * ROLE_SEGS, ROLE_SEGS)] = other.reshape(shape)
    here = pl.ds(offset, block_ref.shape[1])
    copy = pltpu.make_async_copy(block_ref, out_hbm.at[:, here, :], sem)
    copy.start()
    copy.wait()


def finish(own, first, side, second, out, offset, steps_all, after):
    rows, width = own.shape
    steps = rows // ROLE_SEGS
    in_specs = [IN_VMEM] * 4 + [IN_PLACE] * len(after)
    args = [own, first, side, second, *after]
    aliases = {}
    if out is not None:
        in_specs.append(IN_HBM)
        args.append(out)
        aliases = {len(args) - 1: 0}
    return pl.pallas_call(
        functools.partial(finish_kernel, offset),
        in_specs=in_specs,
        out_specs=IN_HBM,
        out_shape=jax.ShapeDtypeStruct((SEGS, steps_all, width), jnp.bfloat16),
        scratch_shapes=[
            pltpu.VMEM((SEGS, steps, width), jnp.bfloat16),
            pltpu.SemaphoreType.DMA,
        ],
        input_output_aliases=aliases,
        compiler_params=params(),
        cost_estimate=cost(FINISH_US),
        name="finish",
    )(*args)


def to_chan(value, target):
    return lax.ppermute(value, "chan", [(i, target(i)) for i in range(8)])


def flip_core(i):
    return i ^ 1


def mate(i):
    return i ^ 2 if i % 2 == 0 else 2 * (3 - i // 2) + 1


def face(i):
    return 2 * (3 - i // 2) if i % 2 == 0 else i ^ 2


def mate_across(i):
    return mate(i ^ 1)


def face_across(i):
    return face(i) ^ 1


def face_other_role(i):
    return face(i ^ 1)


def along_y(value, by):
    return lax.ppermute(
        value, "seq", [(s, s // 4 * 4 + (s % 4 + by) % 4) for s in range(16)]
    )


def around_z(value):
    return lax.ppermute(value, "seq", [(s, (s + 4) % 16) for s in range(16)])


def blocks_decay(rate_ref, block_rows, count):
    return jnp.exp(-rate_ref[...] * (float(block_rows) * count))


def pair_kernel(block_rows, bit, rate_ref, mine_ref, theirs_ref, *refs):
    total_ref, ahead_ref = refs[-2:]
    z, y, chip, core = position()
    second = lax.rem(y if bit == 0 else z, 2) == 1
    mine, theirs = mine_ref[...], theirs_ref[...]
    decay = blocks_decay(rate_ref, block_rows, 1.0)
    total_ref[...] = jnp.where(second, mine + decay * theirs, decay * mine + theirs)
    ahead_ref[...] = jnp.where(second, theirs, 0.0)


def quad_kernel(block_rows, bit, last, rate_ref, mine_ref, theirs_ref, ahead_ref, *refs):
    z, y, chip, core = position()
    at = y if bit == 0 else z
    theirs = theirs_ref[...]
    parity = lax.rem(at, 2).astype(jnp.float32)
    ahead = ahead_ref[...] + jnp.where(
        at >= 2, blocks_decay(rate_ref, block_rows, parity) * theirs, 0.0
    )
    if last:
        row_ahead_ref, out_ref = refs[0], refs[-1]
        within = blocks_decay(rate_ref, block_rows // 4, y.astype(jnp.float32))
        out_ref[...] = row_ahead_ref[...] + within * ahead
    else:
        total_ref, out_ref = refs[-2:]
        mine = mine_ref[...]
        decay = blocks_decay(rate_ref, block_rows, 2.0)
        total_ref[...] = jnp.where(at >= 2, mine + decay * theirs, decay * mine + theirs)
        out_ref[...] = ahead


def state_step(kernel, name, args, after, outputs):
    same = jax.ShapeDtypeStruct(args[0].shape, args[0].dtype)
    return pl.pallas_call(
        kernel,
        in_specs=[IN_VMEM] * len(args) + [IN_PLACE] * len(after),
        out_specs=[IN_VMEM] * outputs,
        out_shape=[same] * outputs,
        compiler_params=params(),
        cost_estimate=cost(ROW_US if name[0] == "r" else COLUMN_US),
        name=name,
    )(*args, *after)


def across(value, bits):
    return lax.ppermute(value, "seq", [(s, s ^ bits) for s in range(16)])


def arriving_state(closing, rate, rows, after):
    part = functools.partial
    pair, ahead = state_step(
        part(pair_kernel, rows, 0), "row_pair", [rate, closing, across(closing, 1)], after[0], 2
    )
    total, row_ahead = state_step(
        part(quad_kernel, rows, 0, False), "row_quad", [rate, pair, across(pair, 2), ahead], after[1], 2
    )
    pair, ahead = state_step(
        part(pair_kernel, 4 * rows, 1), "column_pair", [rate, total, across(total, 4)], after[2], 2
    )
    return state_step(
        part(quad_kernel, 4 * rows, 1, True), "column_quad",
        [rate, pair, across(pair, 8), ahead, row_ahead], after[3], 1,
    )[0]


PARTS = (96, 96)
SEND_US = 0.8
SIDE_US = 0.1
STACK_US = 0.5
ROW_US = 0.5
COLUMN_US = 0.5
DEPS = 'abL'
EARLY = ('', '', 'qQ', 'su')
FINISH_US = 0.4
OWN_US = 2.0


def shards(gate_query, key_proj, value_proj, decay_rates, residues, skip_weight, out_weight):
    rows_here, width_here = key_proj.shape
    steps_all = rows_here // SEGS
    weight = out_weight.reshape(8, width_here, width_here)
    quarters = pick_quarters(weight)
    first_quarter = to_chan(quarters[0], face)
    second_quarter = to_chan(quarters[1], face_other_role)
    p, entry, closing, rate, *for_sibling = closing_pass(
        key_proj, value_proj, decay_rates, weight, quarters[0]
    )
    sibling = [to_chan(piece, flip_core) for piece in for_sibling]
    merged = merge(first_quarter, second_quarter, [])
    early = {"s": sibling[0], "t": sibling[1], "u": sibling[2], "v": sibling[3], "q": first_quarter, "Q": second_quarter, "m": merged}
    after = [[early[c] for c in group] for group in EARLY]
    arriving = arriving_state(closing, rate, rows_here, after)
    quarter = merged
    pieces = [quarter, along_y(quarter, 1), around_z(quarter), along_y(quarter, 3)]
    gain = residues * jnp.sqrt(-jnp.expm1(-2.0 * decay_rates))

    starts = [sum(PARTS[:part]) for part in range(len(PARTS))]
    count = len(PARTS)
    state = entry
    blocks = []
    for part, steps in enumerate(PARTS):
        mine, other, state = gate_pass(
            p, gate_query, rate, gain, skip_weight, state,
            arriving if part == 0 else None, starts[part], steps,
            ([blocks[0][1]] if part == 1 and "a" in DEPS else []) + ([blocks[0][2]] if part == 1 and "b" in DEPS else [])
            + ([merged] if part == 0 and "M" in DEPS else []),
        )
        blocks.append(
            [mine, to_chan(mine, mate), to_chan(other, flip_core), to_chan(other, mate_across)]
        )
    firsts, seconds, sides = [], [], []
    facing = stack_blocks(pieces, [blocks[-1][0]] if "g" in DEPS else [])
    side, first, after = None, None, []
    if "L" not in DEPS:
        side = side_products(blocks[0], sibling, [])
        sides.append(side)
    for part in range(count):
        first, second = send_products(
            blocks[part], facing, [sides[part]] if "V" in DEPS and part < len(sides) else []
        )
        firsts.append(to_chan(first, face))
        seconds.append(to_chan(second, face_across))
        if len(sides) < part + 1:
            pass
        if "L" not in DEPS and part + 1 < count:
            sides.append(side_products(blocks[part + 1], sibling, [first] if "W" in DEPS else []))
    if "L" in DEPS:
        sides = [side_products(blocks[part], sibling, [first]) for part in range(count)]
    sides = [to_chan(side, flip_core) for side in sides]
    out = None
    owns = [own_products(blocks[part], weight, [first] if "K" in DEPS else []) for part in range(count)]
    for part in range(count):
        out = finish(
            owns[part], firsts[part], sides[part], seconds[part], out, starts[part], steps_all, []
        )
    return out.reshape(rows_here, width_here)


def solution(mesh):
    in_specs = (
        P("seq", "chan"),
        P("seq", "chan"),
        P("seq", "chan"),
        P(None, "chan"),
        P(None, "chan"),
        P("chan"),
        P(None, "chan"),
    )
    out_specs = P("seq", "chan")
    return jax.shard_map(shards, mesh=mesh, in_specs=in_specs, out_specs=out_specs, check_vma=False)
```

```python
import functools

import jax
import jax.numpy as jnp
from jax import lax
from jax.experimental import pallas as pl
from jax.experimental.pallas import tpu as pltpu
from jax.sharding import PartitionSpec as P

SEGS = 8
ROLE_SEGS = 4
LANES = 128
LOADS = 4
IN_VMEM = pl.BlockSpec(memory_space=pltpu.VMEM)
IN_SMEM = pl.BlockSpec(memory_space=pltpu.SMEM)
IN_PLACE = pl.BlockSpec(memory_space=pl.ANY)
IN_HBM = pl.BlockSpec(memory_space=pltpu.HBM)


def params(mebibytes=8):
    return pltpu.CompilerParams(vmem_limit_bytes=mebibytes << 20)


def in_hbm(value):
    return pltpu.with_memory_space_constraint(value, pltpu.HBM)


def position():
    seq, chan = lax.axis_index("seq"), lax.axis_index("chan")
    return lax.div(seq, 4), lax.rem(seq, 4), lax.div(chan, 2), lax.rem(chan, 2)


def mate_chip(chip, core):
    return jnp.where(core == 0, jnp.bitwise_xor(chip, 1), 3 - chip)


def face_chip(chip, core):
    return jnp.where(core == 0, 3 - chip, jnp.bitwise_xor(chip, 1))


def depth_block(chip, core, k):
    at_chip = jnp.where(k % 2 == 1, mate_chip(chip, core), chip)
    return 2 * at_chip + jnp.bitwise_xor(core, k // 2)


def own_quarter():
    z, y, chip, core = position()
    return lax.rem(y + 2 * z, 4)


def cost(microseconds):
    return pl.CostEstimate(flops=int(microseconds * 1.15e9), bytes_accessed=0, transcendentals=0)


def spread(row):
    return jnp.broadcast_to(row, (SEGS, LANES))


def tiles(width):
    return [slice(at, at + LANES) for at in range(0, width, LANES)]


def closing_kernel(
    k_hbm, v_hbm, rate_hbm, weight_hbm, quarter_hbm, p_ref, entry_ref, closing_ref, rate_ref,
    sib0_ref, sib1_ref, sib2_ref, sib3_ref, k_buf, v_buf, flat_ref, state_ref, sems, other_sems,
):
    modes, width = rate_ref.shape
    steps = p_ref.shape[0]
    span = steps // LOADS
    stride = span + 1
    rate_copy = pltpu.make_async_copy(rate_hbm, rate_ref, other_sems.at[0])
    rate_copy.start()
    copies = []
    for i in range(LOADS):
        here = pl.ds(i * span, span)
        pair = [
            pltpu.make_async_copy(src.at[:, here, :], buf.at[i], sems.at[which, i])
            for which, (src, buf) in enumerate(((k_hbm, k_buf), (v_hbm, v_buf)))
        ]
        for copy in pair:
            copy.start()
        copies.append(pair)
    z, y, chip, core = position()
    weight_copies = [
        pltpu.make_async_copy(
            weight_hbm.at[depth_block(chip, 1 - core, k)], out_ref, other_sems.at[1 + k]
        )
        for k, out_ref in enumerate((sib0_ref, sib1_ref, sib2_ref, sib3_ref))
    ]
    for copy in weight_copies:
        copy.start()
    rate_copy.wait()
    rate = rate_ref[...]
    pole = jnp.exp(-rate)
    for i in range(LOADS):
        for copy in copies[i]:
            copy.wait()
        for cols in tiles(width):
            for s in range(SEGS):
                flat_ref[s * stride : s * stride + span, :] = k_buf[i, s, :, cols].astype(
                    jnp.float32
                ) * v_buf[i, s, :, cols].astype(jnp.float32)
            poles = [spread(pole[m : m + 1, cols]) for m in range(modes)]

            def step(t, states):
                x = flat_ref[pl.ds(t, SEGS, stride=stride), :]
                p_ref[i * span + t, :, cols] = x
                return tuple(a * s + x for a, s in zip(poles, states))

            if i == 0:
                states = (jnp.zeros((SEGS, LANES), jnp.float32),) * modes
            else:
                states = tuple(state_ref[m, :, cols] for m in range(modes))
            states = lax.fori_loop(0, span, step, states, unroll=UNROLL_CLOSING)
            for m in range(modes):
                state_ref[m, :, cols] = states[m]
    once = jnp.exp(-rate * steps)
    twice = once * once
    hops = ((1, once), (2, twice), (4, twice * twice))
    segment = lax.broadcasted_iota(jnp.int32, (SEGS, LANES), 0)
    for cols in tiles(width):
        for m in range(modes):
            total = state_ref[m, :, cols]
            for hop, decay in hops:
                moved = jnp.where(segment >= hop, pltpu.roll(total, hop, 0), 0.0)
                total = total + spread(decay[m : m + 1, cols]) * moved
            entry_ref[m, :, cols] = jnp.where(segment >= 1, pltpu.roll(total, 1, 0), 0.0)
            closing_ref[m : m + 1, cols] = total[SEGS - 1 :, :]
    for copy in weight_copies:
        copy.wait()


UNROLL_CLOSING = 16
CLOSING_GRANT = 12
CLOSING_US = 5.0
PICK_US = 0.7
MERGE_US = 0.4
GATE_US = 0.8
UNROLL_GATE = 16


def quarter_kernel(weight_hbm, first_ref, second_ref, sems):
    z, y, chip, core = position()
    k = own_quarter()
    copies = []
    for i, out_ref in enumerate((first_ref, second_ref)):
        target = jnp.bitwise_xor(core, i)
        target_chip = face_chip(chip, target)
        at_chip = jnp.where(lax.rem(k, 2) == 1, mate_chip(target_chip, target), target_chip)
        block = 2 * at_chip + jnp.bitwise_xor(target, lax.div(k, 2))
        copies.append(pltpu.make_async_copy(weight_hbm.at[block], out_ref, sems.at[i]))
        copies[i].start()
    for copy in copies:
        copy.wait()


def pick_quarters(weight):
    return pl.pallas_call(
        quarter_kernel,
        in_specs=[IN_HBM],
        out_specs=[IN_VMEM] * 2,
        out_shape=[jax.ShapeDtypeStruct(weight.shape[1:], weight.dtype)] * 2,
        scratch_shapes=[pltpu.SemaphoreType.DMA((2,))],
        compiler_params=params(),
        cost_estimate=cost(PICK_US),
        name="pick_quarters",
    )(in_hbm(weight))


def merge_kernel(first_ref, second_ref, *refs):
    out_ref = refs[-1]
    width = first_ref.shape[1]
    out_ref[:, :width] = first_ref[...]
    out_ref[:, width:] = second_ref[...]


def merge(first, second, after):
    return pl.pallas_call(
        merge_kernel,
        in_specs=[IN_VMEM] * 2 + [IN_PLACE] * len(after),
        out_specs=IN_VMEM,
        out_shape=jax.ShapeDtypeStruct((first.shape[0], 2 * first.shape[1]), first.dtype),
        compiler_params=params(),
        cost_estimate=cost(MERGE_US),
        name="merge",
    )(first, second, *after)


def closing_pass(k, v, rate, weight, quarter):
    rows, width = k.shape
    modes = rate.shape[0]
    steps = rows // SEGS
    span = steps // LOADS
    buffer = pltpu.VMEM((LOADS, SEGS, span, width), k.dtype)
    return pl.pallas_call(
        closing_kernel,
        in_specs=[IN_HBM] * 4 + [IN_PLACE],
        out_specs=[IN_VMEM] * 8,
        out_shape=[
            jax.ShapeDtypeStruct((steps, SEGS, width), jnp.float32),
            jax.ShapeDtypeStruct((modes, SEGS, width), jnp.float32),
            jax.ShapeDtypeStruct((modes, width), jnp.float32),
            jax.ShapeDtypeStruct((modes, width), jnp.float32),
        ]
        + [jax.ShapeDtypeStruct(weight.shape[1:], weight.dtype)] * 4,
        scratch_shapes=[
            buffer,
            buffer,
            pltpu.VMEM((SEGS * (span + 1), LANES), jnp.float32),
            pltpu.VMEM((modes, SEGS, width), jnp.float32),
            pltpu.SemaphoreType.DMA((2, LOADS)),
            pltpu.SemaphoreType.DMA((5,)),
        ],
        compiler_params=params(CLOSING_GRANT),
        cost_estimate=cost(CLOSING_US),
        name="closing_pass",
    )(
        in_hbm(k.reshape(SEGS, steps, width)),
        in_hbm(v.reshape(SEGS, steps, width)),
        in_hbm(rate),
        in_hbm(weight),
        quarter,
    )


def gate_kernel(first, waits, offset, p_ref, q_hbm, rate_ref, gain_ref, skip_ref, *rest):
    arriving_ref = rest[0]
    entry_ref = rest[int(first)]
    mine_ref, other_ref, after_ref, flat_ref, q_buf, sem = rest[int(first) + 1 + waits :]
    modes, width = rate_ref.shape
    steps = mine_ref.shape[0] // ROLE_SEGS
    stride = steps + 1
    fetch = pltpu.make_async_copy(q_hbm.at[:, pl.ds(offset, steps), :], q_buf, sem)
    fetch.start()
    rate = rate_ref[...]
    pole = jnp.exp(-rate)
    if first:
        once = jnp.exp(-rate * p_ref.shape[0])
        twice = once * once
        fourth = twice * twice
        segment = lax.broadcasted_iota(jnp.int32, (SEGS, LANES), 0)
        odd, upper, top = (segment % 2 >= 1, segment % 4 >= 2, segment >= 4)
    for at, cols in enumerate(tiles(width)):
        poles = [spread(pole[m : m + 1, cols]) for m in range(modes)]
        gains = [spread(gain_ref[m : m + 1, cols]) for m in range(modes)]
        skip = spread(skip_ref[:, cols])
        states = []
        for m in range(modes):
            state = entry_ref[m, :, cols]
            if first:
                carried = spread(arriving_ref[m : m + 1, cols])
                for picked, decay in ((odd, once), (upper, twice), (top, fourth)):
                    carried = jnp.where(picked, carried * spread(decay[m : m + 1, cols]), carried)
                state = state + carried
            states.append(state)

        def step(t, states):
            x = p_ref[offset + t, :, cols]
            states = tuple(a * s + x for a, s in zip(poles, states))
            terms = [g * s for g, s in zip(gains, states)] + [skip * x]
            while len(terms) > 1:
                terms = [
                    terms[i] + terms[i + 1] if i + 1 < len(terms) else terms[i]
                    for i in range(0, len(terms), 2)
                ]
            flat_ref[at, pl.ds(t, SEGS, stride=stride), :] = terms[0]
            return states

        states = lax.fori_loop(0, steps, step, tuple(states), unroll=UNROLL_GATE)
        for m in range(modes):
            after_ref[m, :, cols] = states[m]
    fetch.wait()
    z, y, chip, core = position()
    for mine in (0, 1):

        @pl.when(core == mine)
        def _():
            for at, cols in enumerate(tiles(width)):
                for s in range(SEGS):
                    y = flat_ref[at, s * stride : s * stride + steps, :]
                    q = q_buf[s, :, cols].astype(jnp.float32)
                    target = mine_ref if s // ROLE_SEGS == mine else other_ref
                    rows = slice(s % ROLE_SEGS * steps, (s % ROLE_SEGS + 1) * steps)
                    target[rows, cols] = (q * y).astype(jnp.bfloat16)


def gate_pass(p, q, rate, gain, skip, entry, arriving, offset, steps, after):
    steps_all, segs, width = p.shape
    modes = rate.shape[0]
    first = arriving is not None
    args = [p, in_hbm(q.reshape(SEGS, steps_all, width)), rate, gain, skip.reshape(1, width)]
    args += ([arriving] if first else []) + [entry]
    in_specs = [IN_VMEM] * len(args) + [IN_PLACE] * len(after)
    in_specs[1] = IN_HBM
    return pl.pallas_call(
        functools.partial(gate_kernel, first, len(after), offset),
        in_specs=in_specs,
        out_specs=[IN_VMEM] * 3,
        out_shape=[
            jax.ShapeDtypeStruct((ROLE_SEGS * steps, width), jnp.bfloat16),
            jax.ShapeDtypeStruct((ROLE_SEGS * steps, width), jnp.bfloat16),
            jax.ShapeDtypeStruct((modes, SEGS, width), jnp.float32),
        ],
        scratch_shapes=[
            pltpu.VMEM((width // LANES, SEGS * (steps + 1), LANES), jnp.float32),
            pltpu.VMEM((SEGS, steps, width), q.dtype),
            pltpu.SemaphoreType.DMA,
        ],
        compiler_params=params(),
        cost_estimate=cost(GATE_US * steps / 96),
        name="gate_pass",
    )(*args, *after)


def stack_kernel(*refs):
    pieces, out_ref = refs[:4], refs[-1]
    k = own_quarter()
    for i, piece in enumerate(pieces):
        out_ref[lax.rem(k + 4 - i, 4)] = piece[...]


def stack_blocks(pieces, after):
    return pl.pallas_call(
        stack_kernel,
        in_specs=[IN_VMEM] * len(pieces) + [IN_PLACE] * len(after),
        out_specs=IN_VMEM,
        out_shape=jax.ShapeDtypeStruct((len(pieces),) + pieces[0].shape, pieces[0].dtype),
        compiler_params=params(),
        cost_estimate=cost(STACK_US),
        name="stack_blocks",
    )(*pieces, *after)


def send_kernel(*refs):
    blocks, facing_ref, (first_ref, second_ref) = refs[:4], refs[4], refs[-2:]
    width = first_ref.shape[1]
    total = jnp.dot(blocks[0][...], facing_ref[0], preferred_element_type=jnp.float32)
    for k in range(1, 4):
        total += jnp.dot(blocks[k][...], facing_ref[k], preferred_element_type=jnp.float32)
    first_ref[...] = total[:, :width].astype(first_ref.dtype)
    second_ref[...] = total[:, width:].astype(second_ref.dtype)


def send_products(blocks, facing, after):
    rows = blocks[0].shape[0]
    width = facing.shape[2] // 2
    return pl.pallas_call(
        send_kernel,
        in_specs=[IN_VMEM] * 5 + [IN_PLACE] * len(after),
        out_specs=[IN_VMEM] * 2,
        out_shape=[jax.ShapeDtypeStruct((rows, width), jnp.bfloat16)] * 2,
        compiler_params=params(),
        cost_estimate=cost(SEND_US),
        name="send_products",
    )(*blocks, facing, *after)


def side_kernel(*refs):
    blocks, weights, out_ref = refs[:4], refs[4:8], refs[-1]
    total = jnp.dot(blocks[0][...], weights[0][...], preferred_element_type=jnp.float32)
    for k in range(1, 4):
        total += jnp.dot(blocks[k][...], weights[k][...], preferred_element_type=jnp.float32)
    out_ref[...] = total.astype(out_ref.dtype)


def side_products(blocks, sibling, after):
    rows = blocks[0].shape[0]
    width = sibling[0].shape[1]
    return pl.pallas_call(
        side_kernel,
        in_specs=[IN_VMEM] * 8 + [IN_PLACE] * len(after),
        out_specs=IN_VMEM,
        out_shape=jax.ShapeDtypeStruct((rows, width), jnp.bfloat16),
        compiler_params=params(),
        cost_estimate=cost(SIDE_US),
        name="side_products",
    )(*blocks, *sibling, *after)


def own_kernel(*refs):
    blocks, weight_hbm = refs[:4], refs[4]
    out_ref, weight_buf, sems = refs[-3:]
    z, y, chip, core = position()
    fetches = [
        pltpu.make_async_copy(
            weight_hbm.at[depth_block(chip, core, k)], weight_buf.at[k], sems.at[k]
        )
        for k in range(4)
    ]
    for fetch in fetches:
        fetch.start()
    fetches[0].wait()
    total = jnp.dot(blocks[0][...], weight_buf[0], preferred_element_type=jnp.float32)
    for k in range(1, 4):
        fetches[k].wait()
        total += jnp.dot(blocks[k][...], weight_buf[k], preferred_element_type=jnp.float32)
    out_ref[...] = total


def own_products(blocks, weight, after):
    rows, depth = blocks[0].shape
    width = weight.shape[2]
    return pl.pallas_call(
        own_kernel,
        in_specs=[IN_VMEM] * 4 + [IN_HBM] + [IN_PLACE] * len(after),
        out_specs=IN_VMEM,
        out_shape=jax.ShapeDtypeStruct((rows, width), jnp.float32),
        scratch_shapes=[
            pltpu.VMEM((4, depth, width), weight.dtype),
            pltpu.SemaphoreType.DMA((4,)),
        ],
        compiler_params=params(),
        cost_estimate=cost(OWN_US),
        name="own_products",
    )(*blocks, in_hbm(weight), *after)


def finish_kernel(offset, own_ref, first_ref, side_ref, second_ref, *refs):
    out_hbm, block_ref, sem = refs[-3:]
    z, y, chip, core = position()
    shape = (ROLE_SEGS,) + block_ref.shape[1:]
    mine = (own_ref[...] + first_ref[...].astype(jnp.float32)).astype(block_ref.dtype)
    other = (side_ref[...].astype(jnp.float32) + second_ref[...].astype(jnp.float32)).astype(block_ref.dtype)
    block_ref[pl.ds(core * ROLE_SEGS, ROLE_SEGS)] = mine.reshape(shape)
    block_ref[pl.ds((1 - core) * ROLE_SEGS, ROLE_SEGS)] = other.reshape(shape)
    here = pl.ds(offset, block_ref.shape[1])
    copy = pltpu.make_async_copy(block_ref, out_hbm.at[:, here, :], sem)
    copy.start()
    copy.wait()


def finish(own, first, side, second, out, offset, steps_all, after):
    rows, width = own.shape
    steps = rows // ROLE_SEGS
    in_specs = [IN_VMEM] * 4 + [IN_PLACE] * len(after)
    args = [own, first, side, second, *after]
    aliases = {}
    if out is not None:
        in_specs.append(IN_HBM)
        args.append(out)
        aliases = {len(args) - 1: 0}
    return pl.pallas_call(
        functools.partial(finish_kernel, offset),
        in_specs=in_specs,
        out_specs=IN_HBM,
        out_shape=jax.ShapeDtypeStruct((SEGS, steps_all, width), jnp.bfloat16),
        scratch_shapes=[
            pltpu.VMEM((SEGS, steps, width), jnp.bfloat16),
            pltpu.SemaphoreType.DMA,
        ],
        input_output_aliases=aliases,
        compiler_params=params(),
        cost_estimate=cost(FINISH_US),
        name="finish",
    )(*args)


def to_chan(value, target):
    return lax.ppermute(value, "chan", [(i, target(i)) for i in range(8)])


def flip_core(i):
    return i ^ 1


def mate(i):
    return i ^ 2 if i % 2 == 0 else 2 * (3 - i // 2) + 1


def face(i):
    return 2 * (3 - i // 2) if i % 2 == 0 else i ^ 2


def mate_across(i):
    return mate(i ^ 1)


def face_across(i):
    return face(i) ^ 1


def face_other_role(i):
    return face(i ^ 1)


def along_y(value, by):
    return lax.ppermute(
        value, "seq", [(s, s // 4 * 4 + (s % 4 + by) % 4) for s in range(16)]
    )


def around_z(value):
    return lax.ppermute(value, "seq", [(s, (s + 4) % 16) for s in range(16)])


def blocks_decay(rate_ref, block_rows, count):
    return jnp.exp(-rate_ref[...] * (float(block_rows) * count))


def pair_kernel(block_rows, bit, rate_ref, mine_ref, theirs_ref, *refs):
    total_ref, ahead_ref = refs[-2:]
    z, y, chip, core = position()
    second = lax.rem(y if bit == 0 else z, 2) == 1
    mine, theirs = mine_ref[...], theirs_ref[...]
    decay = blocks_decay(rate_ref, block_rows, 1.0)
    total_ref[...] = jnp.where(second, mine + decay * theirs, decay * mine + theirs)
    ahead_ref[...] = jnp.where(second, theirs, 0.0)


def quad_kernel(block_rows, bit, last, rate_ref, mine_ref, theirs_ref, ahead_ref, *refs):
    z, y, chip, core = position()
    at = y if bit == 0 else z
    theirs = theirs_ref[...]
    parity = lax.rem(at, 2).astype(jnp.float32)
    ahead = ahead_ref[...] + jnp.where(
        at >= 2, blocks_decay(rate_ref, block_rows, parity) * theirs, 0.0
    )
    if last:
        row_ahead_ref, out_ref = refs[0], refs[-1]
        within = blocks_decay(rate_ref, block_rows // 4, y.astype(jnp.float32))
        out_ref[...] = row_ahead_ref[...] + within * ahead
    else:
        total_ref, out_ref = refs[-2:]
        mine = mine_ref[...]
        decay = blocks_decay(rate_ref, block_rows, 2.0)
        total_ref[...] = jnp.where(at >= 2, mine + decay * theirs, decay * mine + theirs)
        out_ref[...] = ahead


def state_step(kernel, name, args, after, outputs):
    same = jax.ShapeDtypeStruct(args[0].shape, args[0].dtype)
    return pl.pallas_call(
        kernel,
        in_specs=[IN_VMEM] * len(args) + [IN_PLACE] * len(after),
        out_specs=[IN_VMEM] * outputs,
        out_shape=[same] * outputs,
        compiler_params=params(),
        cost_estimate=cost(ROW_US if name[0] == "r" else COLUMN_US),
        name=name,
    )(*args, *after)


def across(value, bits):
    return lax.ppermute(value, "seq", [(s, s ^ bits) for s in range(16)])


def arriving_state(closing, rate, rows, after):
    part = functools.partial
    pair, ahead = state_step(
        part(pair_kernel, rows, 0), "row_pair", [rate, closing, across(closing, 1)], after[0], 2
    )
    total, row_ahead = state_step(
        part(quad_kernel, rows, 0, False), "row_quad", [rate, pair, across(pair, 2), ahead], after[1], 2
    )
    pair, ahead = state_step(
        part(pair_kernel, 4 * rows, 1), "column_pair", [rate, total, across(total, 4)], after[2], 2
    )
    return state_step(
        part(quad_kernel, 4 * rows, 1, True), "column_quad",
        [rate, pair, across(pair, 8), ahead, row_ahead], after[3], 1,
    )[0]


PARTS = (96, 96)
SEND_US = 0.4
SIDE_US = 0.4
STACK_US = 2.0
ROW_US = 1.5
COLUMN_US = 1.0
DEPS = 'KVWb'
EARLY = ('', 'm', 's', 'qQ')
FINISH_US = 0.4
OWN_US = 0.8


def shards(gate_query, key_proj, value_proj, decay_rates, residues, skip_weight, out_weight):
    rows_here, width_here = key_proj.shape
    steps_all = rows_here // SEGS
    weight = out_weight.reshape(8, width_here, width_here)
    quarters = pick_quarters(weight)
    first_quarter = to_chan(quarters[0], face)
    second_quarter = to_chan(quarters[1], face_other_role)
    p, entry, closing, rate, *for_sibling = closing_pass(
        key_proj, value_proj, decay_rates, weight, quarters[0]
    )
    sibling = [to_chan(piece, flip_core) for piece in for_sibling]
    merged = merge(first_quarter, second_quarter, [])
    early = {"s": sibling[0], "t": sibling[1], "u": sibling[2], "v": sibling[3], "q": first_quarter, "Q": second_quarter, "m": merged}
    after = [[early[c] for c in group] for group in EARLY]
    arriving = arriving_state(closing, rate, rows_here, after)
    quarter = merged
    quarter_after = merge(first_quarter, second_quarter, [arriving])
    pieces = [quarter, along_y(quarter, 1), around_z(quarter_after), along_y(quarter, 3)]
    gain = residues * jnp.sqrt(-jnp.expm1(-2.0 * decay_rates))

    starts = [sum(PARTS[:part]) for part in range(len(PARTS))]
    count = len(PARTS)
    state = entry
    blocks = []
    for part, steps in enumerate(PARTS):
        mine, other, state = gate_pass(
            p, gate_query, rate, gain, skip_weight, state,
            arriving if part == 0 else None, starts[part], steps,
            ([blocks[0][1]] if part == 1 and "a" in DEPS else []) + ([blocks[0][2]] if part == 1 and "b" in DEPS else [])
            + ([merged] if part == 0 and "M" in DEPS else []),
        )
        blocks.append(
            [mine, to_chan(mine, mate), to_chan(other, flip_core), to_chan(other, mate_across)]
        )
    firsts, seconds, sides = [], [], []
    facing = stack_blocks(pieces, [blocks[-1][0]] if "g" in DEPS else [])
    side, first, after = None, None, []
    if "L" not in DEPS:
        side = side_products(blocks[0], sibling, [])
        sides.append(side)
    for part in range(count):
        first, second = send_products(
            blocks[part], facing, [sides[part]] if "V" in DEPS and part < len(sides) else []
        )
        firsts.append(to_chan(first, face))
        seconds.append(to_chan(second, face_across))
        if len(sides) < part + 1:
            pass
        if "L" not in DEPS and part + 1 < count:
            sides.append(side_products(blocks[part + 1], sibling, [first] if "W" in DEPS else []))
    if "L" in DEPS:
        sides = [side_products(blocks[part], sibling, [first]) for part in range(count)]
    sides = [to_chan(side, flip_core) for side in sides]
    out = None
    owns = [own_products(blocks[part], weight, [first] if "K" in DEPS else []) for part in range(count)]
    for part in range(count):
        out = finish(
            owns[part], firsts[part], sides[part], seconds[part], out, starts[part], steps_all, []
        )
    return out.reshape(rows_here, width_here)


def solution(mesh):
    in_specs = (
        P("seq", "chan"),
        P("seq", "chan"),
        P("seq", "chan"),
        P(None, "chan"),
        P(None, "chan"),
        P("chan"),
        P(None, "chan"),
    )
    out_specs = P("seq", "chan")
    return jax.shard_map(shards, mesh=mesh, in_specs=in_specs, out_specs=out_specs, check_vma=False)
```

```python
import functools

import jax
import jax.numpy as jnp
from jax import lax
from jax.experimental import pallas as pl
from jax.experimental.pallas import tpu as pltpu
from jax.sharding import PartitionSpec as P

SEGS = 8
ROLE_SEGS = 4
LANES = 128
LOADS = 4
IN_VMEM = pl.BlockSpec(memory_space=pltpu.VMEM)
IN_SMEM = pl.BlockSpec(memory_space=pltpu.SMEM)
IN_PLACE = pl.BlockSpec(memory_space=pl.ANY)
IN_HBM = pl.BlockSpec(memory_space=pltpu.HBM)


def params(mebibytes=8):
    return pltpu.CompilerParams(vmem_limit_bytes=mebibytes << 20)


def in_hbm(value):
    return pltpu.with_memory_space_constraint(value, pltpu.HBM)


def position():
    seq, chan = lax.axis_index("seq"), lax.axis_index("chan")
    return lax.div(seq, 4), lax.rem(seq, 4), lax.div(chan, 2), lax.rem(chan, 2)


def mate_chip(chip, core):
    return jnp.where(core == 0, jnp.bitwise_xor(chip, 1), 3 - chip)


def face_chip(chip, core):
    return jnp.where(core == 0, 3 - chip, jnp.bitwise_xor(chip, 1))


def depth_block(chip, core, k):
    at_chip = jnp.where(k % 2 == 1, mate_chip(chip, core), chip)
    return 2 * at_chip + jnp.bitwise_xor(core, k // 2)


def own_quarter():
    z, y, chip, core = position()
    return lax.rem(y + 2 * z, 4)


def cost(microseconds):
    return pl.CostEstimate(flops=int(microseconds * 1.15e9), bytes_accessed=0, transcendentals=0)


def spread(row):
    return jnp.broadcast_to(row, (SEGS, LANES))


def tiles(width):
    return [slice(at, at + LANES) for at in range(0, width, LANES)]


def closing_kernel(
    k_hbm, v_hbm, rate_hbm, weight_hbm, p_ref, entry_ref, closing_ref, rate_ref,
    sib0_ref, sib1_ref, sib2_ref, sib3_ref,
    first_ref, second_ref, k_buf, v_buf, flat_ref, state_ref, sems, other_sems,
):
    modes, width = rate_ref.shape
    steps = p_ref.shape[0]
    span = steps // LOADS
    stride = span + 1
    rate_copy = pltpu.make_async_copy(rate_hbm, rate_ref, other_sems.at[0])
    rate_copy.start()
    copies = []
    for i in range(LOADS):
        here = pl.ds(i * span, span)
        pair = [
            pltpu.make_async_copy(src.at[:, here, :], buf.at[i], sems.at[which, i])
            for which, (src, buf) in enumerate(((k_hbm, k_buf), (v_hbm, v_buf)))
        ]
        for copy in pair:
            copy.start()
        copies.append(pair)
    z, y, chip, core = position()
    weight_copies = [
        pltpu.make_async_copy(
            weight_hbm.at[depth_block(chip, 1 - core, k)], out_ref, other_sems.at[1 + k]
        )
        for k, out_ref in enumerate((sib0_ref, sib1_ref, sib2_ref, sib3_ref))
    ]
    quarter = own_quarter()
    for i, out_ref in enumerate((first_ref, second_ref)):
        target = jnp.bitwise_xor(core, i)
        target_chip = face_chip(chip, target)
        at_chip = jnp.where(lax.rem(quarter, 2) == 1, mate_chip(target_chip, target), target_chip)
        block = 2 * at_chip + jnp.bitwise_xor(target, lax.div(quarter, 2))
        weight_copies.append(
            pltpu.make_async_copy(weight_hbm.at[block], out_ref, other_sems.at[5 + i])
        )
    for copy in weight_copies:
        copy.start()
    rate_copy.wait()
    rate = rate_ref[...]
    pole = jnp.exp(-rate)
    for i in range(LOADS):
        for copy in copies[i]:
            copy.wait()
        for cols in tiles(width):
            for s in range(SEGS):
                flat_ref[s * stride : s * stride + span, :] = k_buf[i, s, :, cols].astype(
                    jnp.float32
                ) * v_buf[i, s, :, cols].astype(jnp.float32)
            poles = [spread(pole[m : m + 1, cols]) for m in range(modes)]

            def step(t, states):
                x = flat_ref[pl.ds(t, SEGS, stride=stride), :]
                p_ref[i * span + t, :, cols] = x
                return tuple(a * s + x for a, s in zip(poles, states))

            if i == 0:
                states = (jnp.zeros((SEGS, LANES), jnp.float32),) * modes
            else:
                states = tuple(state_ref[m, :, cols] for m in range(modes))
            states = lax.fori_loop(0, span, step, states, unroll=UNROLL_CLOSING)
            for m in range(modes):
                state_ref[m, :, cols] = states[m]
    once = jnp.exp(-rate * steps)
    twice = once * once
    hops = ((1, once), (2, twice), (4, twice * twice))
    segment = lax.broadcasted_iota(jnp.int32, (SEGS, LANES), 0)
    for cols in tiles(width):
        for m in range(modes):
            total = state_ref[m, :, cols]
            for hop, decay in hops:
                moved = jnp.where(segment >= hop, pltpu.roll(total, hop, 0), 0.0)
                total = total + spread(decay[m : m + 1, cols]) * moved
            entry_ref[m, :, cols] = jnp.where(segment >= 1, pltpu.roll(total, 1, 0), 0.0)
            closing_ref[m : m + 1, cols] = total[SEGS - 1 :, :]
    for copy in weight_copies:
        copy.wait()


UNROLL_CLOSING = 16
CLOSING_GRANT = 12
CLOSING_US = 0.2
MERGE_US = 0.4
GATE_US = 0.8
UNROLL_GATE = 16


def merge_kernel(first_ref, second_ref, *refs):
    out_ref = refs[-1]
    width = first_ref.shape[1]
    out_ref[:, :width] = first_ref[...]
    out_ref[:, width:] = second_ref[...]


def merge(first, second, after):
    return pl.pallas_call(
        merge_kernel,
        in_specs=[IN_VMEM] * 2 + [IN_PLACE] * len(after),
        out_specs=IN_VMEM,
        out_shape=jax.ShapeDtypeStruct((first.shape[0], 2 * first.shape[1]), first.dtype),
        compiler_params=params(),
        cost_estimate=cost(MERGE_US),
        name="merge",
    )(first, second, *after)


def closing_pass(k, v, rate, weight):
    rows, width = k.shape
    modes = rate.shape[0]
    steps = rows // SEGS
    span = steps // LOADS
    buffer = pltpu.VMEM((LOADS, SEGS, span, width), k.dtype)
    return pl.pallas_call(
        closing_kernel,
        in_specs=[IN_HBM] * 4,
        out_specs=[IN_VMEM] * 10,
        out_shape=[
            jax.ShapeDtypeStruct((steps, SEGS, width), jnp.float32),
            jax.ShapeDtypeStruct((modes, SEGS, width), jnp.float32),
            jax.ShapeDtypeStruct((modes, width), jnp.float32),
            jax.ShapeDtypeStruct((modes, width), jnp.float32),
        ]
        + [jax.ShapeDtypeStruct(weight.shape[1:], weight.dtype)] * 6,
        scratch_shapes=[
            buffer,
            buffer,
            pltpu.VMEM((SEGS * (span + 1), LANES), jnp.float32),
            pltpu.VMEM((modes, SEGS, width), jnp.float32),
            pltpu.SemaphoreType.DMA((2, LOADS)),
            pltpu.SemaphoreType.DMA((7,)),
        ],
        compiler_params=params(CLOSING_GRANT),
        cost_estimate=cost(CLOSING_US),
        name="closing_pass",
    )(
        in_hbm(k.reshape(SEGS, steps, width)),
        in_hbm(v.reshape(SEGS, steps, width)),
        in_hbm(rate),
        in_hbm(weight),
    )


def gate_kernel(first, waits, offset, p_ref, q_hbm, rate_ref, gain_ref, skip_ref, *rest):
    arriving_ref = rest[0]
    entry_ref = rest[int(first)]
    mine_ref, other_ref, after_ref, flat_ref, q_buf, sem = rest[int(first) + 1 + waits :]
    modes, width = rate_ref.shape
    steps = mine_ref.shape[0] // ROLE_SEGS
    stride = steps + 1
    fetch = pltpu.make_async_copy(q_hbm.at[:, pl.ds(offset, steps), :], q_buf, sem)
    fetch.start()
    rate = rate_ref[...]
    pole = jnp.exp(-rate)
    if first:
        once = jnp.exp(-rate * p_ref.shape[0])
        twice = once * once
        fourth = twice * twice
        segment = lax.broadcasted_iota(jnp.int32, (SEGS, LANES), 0)
        odd, upper, top = (segment % 2 >= 1, segment % 4 >= 2, segment >= 4)
    for at, cols in enumerate(tiles(width)):
        poles = [spread(pole[m : m + 1, cols]) for m in range(modes)]
        gains = [spread(gain_ref[m : m + 1, cols]) for m in range(modes)]
        skip = spread(skip_ref[:, cols])
        states = []
        for m in range(modes):
            state = entry_ref[m, :, cols]
            if first:
                carried = spread(arriving_ref[m : m + 1, cols])
                for picked, decay in ((odd, once), (upper, twice), (top, fourth)):
                    carried = jnp.where(picked, carried * spread(decay[m : m + 1, cols]), carried)
                state = state + carried
            states.append(state)

        def step(t, states):
            x = p_ref[offset + t, :, cols]
            states = tuple(a * s + x for a, s in zip(poles, states))
            terms = [g * s for g, s in zip(gains, states)] + [skip * x]
            while len(terms) > 1:
                terms = [
                    terms[i] + terms[i + 1] if i + 1 < len(terms) else terms[i]
                    for i in range(0, len(terms), 2)
                ]
            flat_ref[at, pl.ds(t, SEGS, stride=stride), :] = terms[0]
            return states

        states = lax.fori_loop(0, steps, step, tuple(states), unroll=UNROLL_GATE)
        for m in range(modes):
            after_ref[m, :, cols] = states[m]
    fetch.wait()
    z, y, chip, core = position()
    for mine in (0, 1):

        @pl.when(core == mine)
        def _():
            for at, cols in enumerate(tiles(width)):
                for s in range(SEGS):
                    y = flat_ref[at, s * stride : s * stride + steps, :]
                    q = q_buf[s, :, cols].astype(jnp.float32)
                    target = mine_ref if s // ROLE_SEGS == mine else other_ref
                    rows = slice(s % ROLE_SEGS * steps, (s % ROLE_SEGS + 1) * steps)
                    target[rows, cols] = (q * y).astype(jnp.bfloat16)


def gate_pass(p, q, rate, gain, skip, entry, arriving, offset, steps, after):
    steps_all, segs, width = p.shape
    modes = rate.shape[0]
    first = arriving is not None
    args = [p, in_hbm(q.reshape(SEGS, steps_all, width)), rate, gain, skip.reshape(1, width)]
    args += ([arriving] if first else []) + [entry]
    in_specs = [IN_VMEM] * len(args) + [IN_PLACE] * len(after)
    in_specs[1] = IN_HBM
    return pl.pallas_call(
        functools.partial(gate_kernel, first, len(after), offset),
        in_specs=in_specs,
        out_specs=[IN_VMEM] * 3,
        out_shape=[
            jax.ShapeDtypeStruct((ROLE_SEGS * steps, width), jnp.bfloat16),
            jax.ShapeDtypeStruct((ROLE_SEGS * steps, width), jnp.bfloat16),
            jax.ShapeDtypeStruct((modes, SEGS, width), jnp.float32),
        ],
        scratch_shapes=[
            pltpu.VMEM((width // LANES, SEGS * (steps + 1), LANES), jnp.float32),
            pltpu.VMEM((SEGS, steps, width), q.dtype),
            pltpu.SemaphoreType.DMA,
        ],
        compiler_params=params(),
        cost_estimate=cost(GATE_US * steps / 96),
        name="gate_pass",
    )(*args, *after)


def stack_kernel(*refs):
    pieces, out_ref = refs[:4], refs[-1]
    k = own_quarter()
    for i, piece in enumerate(pieces):
        out_ref[lax.rem(k + 4 - i, 4)] = piece[...]


def stack_blocks(pieces, after):
    return pl.pallas_call(
        stack_kernel,
        in_specs=[IN_VMEM] * len(pieces) + [IN_PLACE] * len(after),
        out_specs=IN_VMEM,
        out_shape=jax.ShapeDtypeStruct((len(pieces),) + pieces[0].shape, pieces[0].dtype),
        compiler_params=params(),
        cost_estimate=cost(STACK_US),
        name="stack_blocks",
    )(*pieces, *after)


def send_kernel(*refs):
    blocks, facing_ref, (first_ref, second_ref) = refs[:4], refs[4], refs[-2:]
    width = first_ref.shape[1]
    total = jnp.dot(blocks[0][...], facing_ref[0], preferred_element_type=jnp.float32)
    for k in range(1, 4):
        total += jnp.dot(blocks[k][...], facing_ref[k], preferred_element_type=jnp.float32)
    first_ref[...] = total[:, :width].astype(first_ref.dtype)
    second_ref[...] = total[:, width:].astype(second_ref.dtype)


def send_products(blocks, facing, after):
    rows = blocks[0].shape[0]
    width = facing.shape[2] // 2
    return pl.pallas_call(
        send_kernel,
        in_specs=[IN_VMEM] * 5 + [IN_PLACE] * len(after),
        out_specs=[IN_VMEM] * 2,
        out_shape=[jax.ShapeDtypeStruct((rows, width), jnp.bfloat16)] * 2,
        compiler_params=params(),
        cost_estimate=cost(SEND_US),
        name="send_products",
    )(*blocks, facing, *after)


def side_kernel(*refs):
    blocks, weights, out_ref = refs[:4], refs[4:8], refs[-1]
    total = jnp.dot(blocks[0][...], weights[0][...], preferred_element_type=jnp.float32)
    for k in range(1, 4):
        total += jnp.dot(blocks[k][...], weights[k][...], preferred_element_type=jnp.float32)
    out_ref[...] = total.astype(out_ref.dtype)


def side_products(blocks, sibling, after):
    rows = blocks[0].shape[0]
    width = sibling[0].shape[1]
    return pl.pallas_call(
        side_kernel,
        in_specs=[IN_VMEM] * 8 + [IN_PLACE] * len(after),
        out_specs=IN_VMEM,
        out_shape=jax.ShapeDtypeStruct((rows, width), jnp.bfloat16),
        compiler_params=params(),
        cost_estimate=cost(SIDE_US),
        name="side_products",
    )(*blocks, *sibling, *after)


def own_kernel(*refs):
    blocks, weight_hbm = refs[:4], refs[4]
    out_ref, weight_buf, sems = refs[-3:]
    z, y, chip, core = position()
    fetches = [
        pltpu.make_async_copy(
            weight_hbm.at[depth_block(chip, core, k)], weight_buf.at[k], sems.at[k]
        )
        for k in range(4)
    ]
    for fetch in fetches:
        fetch.start()
    fetches[0].wait()
    total = jnp.dot(blocks[0][...], weight_buf[0], preferred_element_type=jnp.float32)
    for k in range(1, 4):
        fetches[k].wait()
        total += jnp.dot(blocks[k][...], weight_buf[k], preferred_element_type=jnp.float32)
    out_ref[...] = total


def own_products(blocks, weight, after):
    rows, depth = blocks[0].shape
    width = weight.shape[2]
    return pl.pallas_call(
        own_kernel,
        in_specs=[IN_VMEM] * 4 + [IN_HBM] + [IN_PLACE] * len(after),
        out_specs=IN_VMEM,
        out_shape=jax.ShapeDtypeStruct((rows, width), jnp.float32),
        scratch_shapes=[
            pltpu.VMEM((4, depth, width), weight.dtype),
            pltpu.SemaphoreType.DMA((4,)),
        ],
        compiler_params=params(),
        cost_estimate=cost(OWN_US),
        name="own_products",
    )(*blocks, in_hbm(weight), *after)


def finish_kernel(offset, own_ref, first_ref, side_ref, second_ref, *refs):
    out_hbm, block_ref, sem = refs[-3:]
    z, y, chip, core = position()
    here = pl.ds(offset, block_ref.shape[2])
    copies = []
    for i, (kept_ref, sent_ref) in enumerate(((own_ref, first_ref), (side_ref, second_ref))):
        total = kept_ref[...].astype(jnp.float32) + sent_ref[...].astype(jnp.float32)
        block_ref[i] = total.astype(block_ref.dtype).reshape(block_ref.shape[1:])
        segments = pl.ds(jnp.bitwise_xor(core, i) * ROLE_SEGS, ROLE_SEGS)
        copies.append(
            pltpu.make_async_copy(block_ref.at[i], out_hbm.at[segments, here, :], sem.at[i])
        )
        copies[i].start()
    for copy in copies:
        copy.wait()


def finish(own, first, side, second, out, offset, steps_all, after):
    rows, width = own.shape
    steps = rows // ROLE_SEGS
    in_specs = [IN_VMEM] * 4 + [IN_PLACE] * len(after)
    args = [own, first, side, second, *after]
    aliases = {}
    if out is not None:
        in_specs.append(IN_HBM)
        args.append(out)
        aliases = {len(args) - 1: 0}
    return pl.pallas_call(
        functools.partial(finish_kernel, offset),
        in_specs=in_specs,
        out_specs=IN_HBM,
        out_shape=jax.ShapeDtypeStruct((SEGS, steps_all, width), jnp.bfloat16),
        scratch_shapes=[
            pltpu.VMEM((2, ROLE_SEGS, steps, width), jnp.bfloat16),
            pltpu.SemaphoreType.DMA((2,)),
        ],
        input_output_aliases=aliases,
        compiler_params=params(),
        cost_estimate=cost(FINISH_US),
        name="finish",
    )(*args)


def to_chan(value, target):
    return lax.ppermute(value, "chan", [(i, target(i)) for i in range(8)])


def flip_core(i):
    return i ^ 1


def mate(i):
    return i ^ 2 if i % 2 == 0 else 2 * (3 - i // 2) + 1


def face(i):
    return 2 * (3 - i // 2) if i % 2 == 0 else i ^ 2


def mate_across(i):
    return mate(i ^ 1)


def face_across(i):
    return face(i) ^ 1


def face_other_role(i):
    return face(i ^ 1)


def along_y(value, by):
    return lax.ppermute(
        value, "seq", [(s, s // 4 * 4 + (s % 4 + by) % 4) for s in range(16)]
    )


def around_z(value):
    return lax.ppermute(value, "seq", [(s, (s + 4) % 16) for s in range(16)])


def blocks_decay(rate_ref, block_rows, count):
    return jnp.exp(-rate_ref[...] * (float(block_rows) * count))


def pair_kernel(block_rows, bit, rate_ref, mine_ref, theirs_ref, *refs):
    total_ref, ahead_ref = refs[-2:]
    z, y, chip, core = position()
    second = lax.rem(y if bit == 0 else z, 2) == 1
    mine, theirs = mine_ref[...], theirs_ref[...]
    decay = blocks_decay(rate_ref, block_rows, 1.0)
    total_ref[...] = jnp.where(second, mine + decay * theirs, decay * mine + theirs)
    ahead_ref[...] = jnp.where(second, theirs, 0.0)


def quad_kernel(block_rows, bit, last, rate_ref, mine_ref, theirs_ref, ahead_ref, *refs):
    z, y, chip, core = position()
    at = y if bit == 0 else z
    theirs = theirs_ref[...]
    parity = lax.rem(at, 2).astype(jnp.float32)
    ahead = ahead_ref[...] + jnp.where(
        at >= 2, blocks_decay(rate_ref, block_rows, parity) * theirs, 0.0
    )
    if last:
        row_ahead_ref, out_ref = refs[0], refs[-1]
        within = blocks_decay(rate_ref, block_rows // 4, y.astype(jnp.float32))
        out_ref[...] = row_ahead_ref[...] + within * ahead
    else:
        total_ref, out_ref = refs[-2:]
        mine = mine_ref[...]
        decay = blocks_decay(rate_ref, block_rows, 2.0)
        total_ref[...] = jnp.where(at >= 2, mine + decay * theirs, decay * mine + theirs)
        out_ref[...] = ahead


def state_step(kernel, name, args, after, outputs):
    same = jax.ShapeDtypeStruct(args[0].shape, args[0].dtype)
    return pl.pallas_call(
        kernel,
        in_specs=[IN_VMEM] * len(args) + [IN_PLACE] * len(after),
        out_specs=[IN_VMEM] * outputs,
        out_shape=[same] * outputs,
        compiler_params=params(),
        cost_estimate=cost(ROW_US if name[0] == "r" else COLUMN_US),
        name=name,
    )(*args, *after)


def across(value, bits):
    return lax.ppermute(value, "seq", [(s, s ^ bits) for s in range(16)])


def arriving_state(closing, rate, rows, after):
    part = functools.partial
    pair, ahead = state_step(
        part(pair_kernel, rows, 0), "row_pair", [rate, closing, across(closing, 1)], after[0], 2
    )
    total, row_ahead = state_step(
        part(quad_kernel, rows, 0, False), "row_quad", [rate, pair, across(pair, 2), ahead], after[1], 2
    )
    pair, ahead = state_step(
        part(pair_kernel, 4 * rows, 1), "column_pair", [rate, total, across(total, 4)], after[2], 2
    )
    return state_step(
        part(quad_kernel, 4 * rows, 1, True), "column_quad",
        [rate, pair, across(pair, 8), ahead, row_ahead], after[3], 1,
    )[0]


PARTS = (96, 96)
SEND_US = 0.4
SIDE_US = 0.4
STACK_US = 2.0
ROW_US = 1.5
COLUMN_US = 1.0
DEPS = 'bVWK'
EARLY = ('', '', 'q', 'sQ')
FINISH_US = 0.4
OWN_US = 0.8


def shards(gate_query, key_proj, value_proj, decay_rates, residues, skip_weight, out_weight):
    rows_here, width_here = key_proj.shape
    steps_all = rows_here // SEGS
    weight = out_weight.reshape(8, width_here, width_here)
    p, entry, closing, rate, *pieces = closing_pass(key_proj, value_proj, decay_rates, weight)
    for_sibling, quarters = pieces[:4], pieces[4:]
    first_quarter = to_chan(quarters[0], face)
    second_quarter = to_chan(quarters[1], face_other_role)
    sibling = [to_chan(piece, flip_core) for piece in for_sibling]
    merged = merge(first_quarter, second_quarter, [])
    early = {"s": sibling[0], "t": sibling[1], "u": sibling[2], "v": sibling[3], "q": first_quarter, "Q": second_quarter, "m": merged}
    after = [[early[c] for c in group] for group in EARLY]
    arriving = arriving_state(closing, rate, rows_here, after)
    quarter = merged
    quarter_after = merge(first_quarter, second_quarter, [arriving])
    pieces = [quarter, along_y(quarter, 1), around_z(quarter_after), along_y(quarter, 3)]
    gain = residues * jnp.sqrt(-jnp.expm1(-2.0 * decay_rates))

    starts = [sum(PARTS[:part]) for part in range(len(PARTS))]
    count = len(PARTS)
    state = entry
    blocks = []
    for part, steps in enumerate(PARTS):
        mine, other, state = gate_pass(
            p, gate_query, rate, gain, skip_weight, state,
            arriving if part == 0 else None, starts[part], steps,
            ([blocks[0][1]] if part == 1 and "a" in DEPS else []) + ([blocks[0][2]] if part == 1 and "b" in DEPS else [])
            + ([merged] if part == 0 and "M" in DEPS else []),
        )
        blocks.append(
            [mine, to_chan(mine, mate), to_chan(other, flip_core), to_chan(other, mate_across)]
        )
    firsts, seconds, sides = [], [], []
    facing = stack_blocks(pieces, [blocks[-1][0]] if "g" in DEPS else [])
    side, first, after = None, None, []
    if "L" not in DEPS:
        side = side_products(blocks[0], sibling, [])
        sides.append(side)
    for part in range(count):
        first, second = send_products(
            blocks[part], facing, [sides[part]] if "V" in DEPS and part < len(sides) else []
        )
        firsts.append(to_chan(first, face))
        seconds.append(to_chan(second, face_across))
        if len(sides) < part + 1:
            pass
        if "L" not in DEPS and part + 1 < count:
            sides.append(side_products(blocks[part + 1], sibling, [first] if "W" in DEPS else []))
    if "L" in DEPS:
        sides = [side_products(blocks[part], sibling, [first]) for part in range(count)]
    sides = [to_chan(side, flip_core) for side in sides]
    out = None
    owns = [own_products(blocks[part], weight, [first] if "K" in DEPS else []) for part in range(count)]
    for part in range(count):
        out = finish(
            owns[part], firsts[part], sides[part], seconds[part], out, starts[part], steps_all, []
        )
    return out.reshape(rows_here, width_here)


def solution(mesh):
    in_specs = (
        P("seq", "chan"),
        P("seq", "chan"),
        P("seq", "chan"),
        P(None, "chan"),
        P(None, "chan"),
        P("chan"),
        P(None, "chan"),
    )
    out_specs = P("seq", "chan")
    return jax.shard_map(shards, mesh=mesh, in_specs=in_specs, out_specs=out_specs, check_vma=False)
```

```python
import functools

import jax
import jax.numpy as jnp
from jax import lax
from jax.experimental import pallas as pl
from jax.experimental.pallas import tpu as pltpu
from jax.sharding import PartitionSpec as P

SEGS = 8
ROLE_SEGS = 4
LANES = 128
LOADS = 4
IN_VMEM = pl.BlockSpec(memory_space=pltpu.VMEM)
IN_SMEM = pl.BlockSpec(memory_space=pltpu.SMEM)
IN_PLACE = pl.BlockSpec(memory_space=pl.ANY)
IN_HBM = pl.BlockSpec(memory_space=pltpu.HBM)


def params(mebibytes=8):
    return pltpu.CompilerParams(vmem_limit_bytes=mebibytes << 20)


def in_hbm(value):
    return pltpu.with_memory_space_constraint(value, pltpu.HBM)


def position():
    seq, chan = lax.axis_index("seq"), lax.axis_index("chan")
    return lax.div(seq, 4), lax.rem(seq, 4), lax.div(chan, 2), lax.rem(chan, 2)


def mate_chip(chip, core):
    return jnp.where(core == 0, jnp.bitwise_xor(chip, 1), 3 - chip)


def face_chip(chip, core):
    return jnp.where(core == 0, 3 - chip, jnp.bitwise_xor(chip, 1))


def depth_block(chip, core, k):
    at_chip = jnp.where(k % 2 == 1, mate_chip(chip, core), chip)
    return 2 * at_chip + jnp.bitwise_xor(core, k // 2)


def own_quarter():
    z, y, chip, core = position()
    return lax.rem(y + 2 * z, 4)


def cost(microseconds):
    return pl.CostEstimate(flops=int(microseconds * 1.15e9), bytes_accessed=0, transcendentals=0)


def spread(row):
    return jnp.broadcast_to(row, (SEGS, LANES))


def tiles(width):
    return [slice(at, at + LANES) for at in range(0, width, LANES)]


def closing_kernel(
    k_hbm, v_hbm, rate_hbm, weight_hbm, p_ref, entry_ref, closing_ref, rate_ref,
    sib0_ref, sib1_ref, sib2_ref, sib3_ref,
    first_ref, second_ref, k_buf, v_buf, flat_ref, state_ref, sems, other_sems,
):
    modes, width = rate_ref.shape
    steps = p_ref.shape[0]
    span = steps // LOADS
    stride = span + 1
    rate_copy = pltpu.make_async_copy(rate_hbm, rate_ref, other_sems.at[0])
    rate_copy.start()
    copies = []
    for i in range(LOADS):
        here = pl.ds(i * span, span)
        pair = [
            pltpu.make_async_copy(src.at[:, here, :], buf.at[i], sems.at[which, i])
            for which, (src, buf) in enumerate(((k_hbm, k_buf), (v_hbm, v_buf)))
        ]
        for copy in pair:
            copy.start()
        copies.append(pair)
    z, y, chip, core = position()
    weight_copies = [
        pltpu.make_async_copy(
            weight_hbm.at[depth_block(chip, 1 - core, k)], out_ref, other_sems.at[1 + k]
        )
        for k, out_ref in enumerate((sib0_ref, sib1_ref, sib2_ref, sib3_ref))
    ]
    quarter = own_quarter()
    for i, out_ref in enumerate((first_ref, second_ref)):
        target = jnp.bitwise_xor(core, i)
        target_chip = face_chip(chip, target)
        at_chip = jnp.where(lax.rem(quarter, 2) == 1, mate_chip(target_chip, target), target_chip)
        block = 2 * at_chip + jnp.bitwise_xor(target, lax.div(quarter, 2))
        weight_copies.append(
            pltpu.make_async_copy(weight_hbm.at[block], out_ref, other_sems.at[5 + i])
        )
    for copy in weight_copies:
        copy.start()
    rate_copy.wait()
    rate = rate_ref[...]
    pole = jnp.exp(-rate)
    for i in range(LOADS):
        for copy in copies[i]:
            copy.wait()
        for cols in tiles(width):
            for s in range(SEGS):
                flat_ref[s * stride : s * stride + span, :] = k_buf[i, s, :, cols].astype(
                    jnp.float32
                ) * v_buf[i, s, :, cols].astype(jnp.float32)
            poles = [spread(pole[m : m + 1, cols]) for m in range(modes)]

            def step(t, states):
                x = flat_ref[pl.ds(t, SEGS, stride=stride), :]
                p_ref[i * span + t, :, cols] = x
                return tuple(a * s + x for a, s in zip(poles, states))

            if i == 0:
                states = (jnp.zeros((SEGS, LANES), jnp.float32),) * modes
            else:
                states = tuple(state_ref[m, :, cols] for m in range(modes))
            states = lax.fori_loop(0, span, step, states, unroll=UNROLL_CLOSING)
            for m in range(modes):
                state_ref[m, :, cols] = states[m]
    once = jnp.exp(-rate * steps)
    twice = once * once
    hops = ((1, once), (2, twice), (4, twice * twice))
    segment = lax.broadcasted_iota(jnp.int32, (SEGS, LANES), 0)
    for cols in tiles(width):
        for m in range(modes):
            total = state_ref[m, :, cols]
            for hop, decay in hops:
                moved = jnp.where(segment >= hop, pltpu.roll(total, hop, 0), 0.0)
                total = total + spread(decay[m : m + 1, cols]) * moved
            entry_ref[m, :, cols] = jnp.where(segment >= 1, pltpu.roll(total, 1, 0), 0.0)
            closing_ref[m : m + 1, cols] = total[SEGS - 1 :, :]
    for copy in weight_copies:
        copy.wait()


UNROLL_CLOSING = 16
CLOSING_GRANT = 12
CLOSING_US = 1.0
MERGE_US = 0.4
GATE_US = 0.8
UNROLL_GATE = 16


def merge_kernel(first_ref, second_ref, *refs):
    out_ref = refs[-1]
    width = first_ref.shape[1]
    out_ref[:, :width] = first_ref[...]
    out_ref[:, width:] = second_ref[...]


def merge(first, second, after):
    return pl.pallas_call(
        merge_kernel,
        in_specs=[IN_VMEM] * 2 + [IN_PLACE] * len(after),
        out_specs=IN_VMEM,
        out_shape=jax.ShapeDtypeStruct((first.shape[0], 2 * first.shape[1]), first.dtype),
        compiler_params=params(),
        cost_estimate=cost(MERGE_US),
        name="merge",
    )(first, second, *after)


def closing_pass(k, v, rate, weight):
    rows, width = k.shape
    modes = rate.shape[0]
    steps = rows // SEGS
    span = steps // LOADS
    buffer = pltpu.VMEM((LOADS, SEGS, span, width), k.dtype)
    return pl.pallas_call(
        closing_kernel,
        in_specs=[IN_HBM] * 4,
        out_specs=[IN_VMEM] * 10,
        out_shape=[
            jax.ShapeDtypeStruct((steps, SEGS, width), jnp.float32),
            jax.ShapeDtypeStruct((modes, SEGS, width), jnp.float32),
            jax.ShapeDtypeStruct((modes, width), jnp.float32),
            jax.ShapeDtypeStruct((modes, width), jnp.float32),
        ]
        + [jax.ShapeDtypeStruct(weight.shape[1:], weight.dtype)] * 6,
        scratch_shapes=[
            buffer,
            buffer,
            pltpu.VMEM((SEGS * (span + 1), LANES), jnp.float32),
            pltpu.VMEM((modes, SEGS, width), jnp.float32),
            pltpu.SemaphoreType.DMA((2, LOADS)),
            pltpu.SemaphoreType.DMA((7,)),
        ],
        compiler_params=params(CLOSING_GRANT),
        cost_estimate=cost(CLOSING_US),
        name="closing_pass",
    )(
        in_hbm(k.reshape(SEGS, steps, width)),
        in_hbm(v.reshape(SEGS, steps, width)),
        in_hbm(rate),
        in_hbm(weight),
    )


def gate_kernel(first, waits, offset, p_ref, q_hbm, rate_ref, gain_ref, skip_ref, *rest):
    arriving_ref = rest[0]
    entry_ref = rest[int(first)]
    mine_ref, other_ref, after_ref, flat_ref, q_buf, sem = rest[int(first) + 1 + waits :]
    modes, width = rate_ref.shape
    steps = mine_ref.shape[0] // ROLE_SEGS
    stride = steps + 1
    fetch = pltpu.make_async_copy(q_hbm.at[:, pl.ds(offset, steps), :], q_buf, sem)
    fetch.start()
    rate = rate_ref[...]
    pole = jnp.exp(-rate)
    if first:
        once = jnp.exp(-rate * p_ref.shape[0])
        twice = once * once
        fourth = twice * twice
        segment = lax.broadcasted_iota(jnp.int32, (SEGS, LANES), 0)
        odd, upper, top = (segment % 2 >= 1, segment % 4 >= 2, segment >= 4)
    for at, cols in enumerate(tiles(width)):
        poles = [spread(pole[m : m + 1, cols]) for m in range(modes)]
        gains = [spread(gain_ref[m : m + 1, cols]) for m in range(modes)]
        skip = spread(skip_ref[:, cols])
        states = []
        for m in range(modes):
            state = entry_ref[m, :, cols]
            if first:
                carried = spread(arriving_ref[m : m + 1, cols])
                for picked, decay in ((odd, once), (upper, twice), (top, fourth)):
                    carried = jnp.where(picked, carried * spread(decay[m : m + 1, cols]), carried)
                state = state + carried
            states.append(state)

        def step(t, states):
            x = p_ref[offset + t, :, cols]
            states = tuple(a * s + x for a, s in zip(poles, states))
            terms = [g * s for g, s in zip(gains, states)] + [skip * x]
            while len(terms) > 1:
                terms = [
                    terms[i] + terms[i + 1] if i + 1 < len(terms) else terms[i]
                    for i in range(0, len(terms), 2)
                ]
            flat_ref[at, pl.ds(t, SEGS, stride=stride), :] = terms[0]
            return states

        states = lax.fori_loop(0, steps, step, tuple(states), unroll=UNROLL_GATE)
        for m in range(modes):
            after_ref[m, :, cols] = states[m]
    fetch.wait()
    z, y, chip, core = position()
    for mine in (0, 1):

        @pl.when(core == mine)
        def _():
            for at, cols in enumerate(tiles(width)):
                for s in range(SEGS):
                    y = flat_ref[at, s * stride : s * stride + steps, :]
                    q = q_buf[s, :, cols].astype(jnp.float32)
                    target = mine_ref if s // ROLE_SEGS == mine else other_ref
                    rows = slice(s % ROLE_SEGS * steps, (s % ROLE_SEGS + 1) * steps)
                    target[rows, cols] = (q * y).astype(jnp.bfloat16)


def gate_pass(p, q, rate, gain, skip, entry, arriving, offset, steps, after):
    steps_all, segs, width = p.shape
    modes = rate.shape[0]
    first = arriving is not None
    args = [p, in_hbm(q.reshape(SEGS, steps_all, width)), rate, gain, skip.reshape(1, width)]
    args += ([arriving] if first else []) + [entry]
    in_specs = [IN_VMEM] * len(args) + [IN_PLACE] * len(after)
    in_specs[1] = IN_HBM
    return pl.pallas_call(
        functools.partial(gate_kernel, first, len(after), offset),
        in_specs=in_specs,
        out_specs=[IN_VMEM] * 3,
        out_shape=[
            jax.ShapeDtypeStruct((ROLE_SEGS * steps, width), jnp.bfloat16),
            jax.ShapeDtypeStruct((ROLE_SEGS * steps, width), jnp.bfloat16),
            jax.ShapeDtypeStruct((modes, SEGS, width), jnp.float32),
        ],
        scratch_shapes=[
            pltpu.VMEM((width // LANES, SEGS * (steps + 1), LANES), jnp.float32),
            pltpu.VMEM((SEGS, steps, width), q.dtype),
            pltpu.SemaphoreType.DMA,
        ],
        compiler_params=params(),
        cost_estimate=cost(GATE_US * steps / 96),
        name="gate_pass",
    )(*args, *after)


def stack_kernel(*refs):
    pieces, out_ref = refs[:4], refs[-1]
    k = own_quarter()
    for i, piece in enumerate(pieces):
        out_ref[lax.rem(k + 4 - i, 4)] = piece[...]


def stack_blocks(pieces, after):
    return pl.pallas_call(
        stack_kernel,
        in_specs=[IN_VMEM] * len(pieces) + [IN_PLACE] * len(after),
        out_specs=IN_VMEM,
        out_shape=jax.ShapeDtypeStruct((len(pieces),) + pieces[0].shape, pieces[0].dtype),
        compiler_params=params(),
        cost_estimate=cost(STACK_US),
        name="stack_blocks",
    )(*pieces, *after)


def send_kernel(*refs):
    blocks, facing_ref, (first_ref, second_ref) = refs[:4], refs[4], refs[-2:]
    width = first_ref.shape[1]
    total = jnp.dot(blocks[0][...], facing_ref[0], preferred_element_type=jnp.float32)
    for k in range(1, 4):
        total += jnp.dot(blocks[k][...], facing_ref[k], preferred_element_type=jnp.float32)
    first_ref[...] = total[:, :width].astype(first_ref.dtype)
    second_ref[...] = total[:, width:].astype(second_ref.dtype)


def send_products(blocks, facing, after):
    rows = blocks[0].shape[0]
    width = facing.shape[2] // 2
    return pl.pallas_call(
        send_kernel,
        in_specs=[IN_VMEM] * 5 + [IN_PLACE] * len(after),
        out_specs=[IN_VMEM] * 2,
        out_shape=[jax.ShapeDtypeStruct((rows, width), jnp.bfloat16)] * 2,
        compiler_params=params(),
        cost_estimate=cost(SEND_US),
        name="send_products",
    )(*blocks, facing, *after)


def side_kernel(*refs):
    blocks, weights, out_ref = refs[:4], refs[4:8], refs[-1]
    total = jnp.dot(blocks[0][...], weights[0][...], preferred_element_type=jnp.float32)
    for k in range(1, 4):
        total += jnp.dot(blocks[k][...], weights[k][...], preferred_element_type=jnp.float32)
    out_ref[...] = total.astype(out_ref.dtype)


def side_products(blocks, sibling, after):
    rows = blocks[0].shape[0]
    width = sibling[0].shape[1]
    return pl.pallas_call(
        side_kernel,
        in_specs=[IN_VMEM] * 8 + [IN_PLACE] * len(after),
        out_specs=IN_VMEM,
        out_shape=jax.ShapeDtypeStruct((rows, width), jnp.bfloat16),
        compiler_params=params(),
        cost_estimate=cost(SIDE_US),
        name="side_products",
    )(*blocks, *sibling, *after)


def own_kernel(*refs):
    blocks, weight_hbm = refs[:4], refs[4]
    out_ref, weight_buf, sems = refs[-3:]
    z, y, chip, core = position()
    fetches = [
        pltpu.make_async_copy(
            weight_hbm.at[depth_block(chip, core, k)], weight_buf.at[k], sems.at[k]
        )
        for k in range(4)
    ]
    for fetch in fetches:
        fetch.start()
    fetches[0].wait()
    total = jnp.dot(blocks[0][...], weight_buf[0], preferred_element_type=jnp.float32)
    for k in range(1, 4):
        fetches[k].wait()
        total += jnp.dot(blocks[k][...], weight_buf[k], preferred_element_type=jnp.float32)
    out_ref[...] = total


def own_products(blocks, weight, after):
    rows, depth = blocks[0].shape
    width = weight.shape[2]
    return pl.pallas_call(
        own_kernel,
        in_specs=[IN_VMEM] * 4 + [IN_HBM] + [IN_PLACE] * len(after),
        out_specs=IN_VMEM,
        out_shape=jax.ShapeDtypeStruct((rows, width), jnp.float32),
        scratch_shapes=[
            pltpu.VMEM((4, depth, width), weight.dtype),
            pltpu.SemaphoreType.DMA((4,)),
        ],
        compiler_params=params(),
        cost_estimate=cost(OWN_US),
        name="own_products",
    )(*blocks, in_hbm(weight), *after)


def finish_kernel(offset, own_ref, first_ref, side_ref, second_ref, *refs):
    out_hbm, block_ref, sem = refs[-3:]
    z, y, chip, core = position()
    here = pl.ds(offset, block_ref.shape[2])
    copies = []
    for i, (kept_ref, sent_ref) in enumerate(((own_ref, first_ref), (side_ref, second_ref))):
        total = kept_ref[...].astype(jnp.float32) + sent_ref[...].astype(jnp.float32)
        block_ref[i] = total.astype(block_ref.dtype).reshape(block_ref.shape[1:])
        segments = pl.ds(jnp.bitwise_xor(core, i) * ROLE_SEGS, ROLE_SEGS)
        copies.append(
            pltpu.make_async_copy(block_ref.at[i], out_hbm.at[segments, here, :], sem.at[i])
        )
        copies[i].start()
    for copy in copies:
        copy.wait()


def finish(own, first, side, second, out, offset, steps_all, after):
    rows, width = own.shape
    steps = rows // ROLE_SEGS
    in_specs = [IN_VMEM] * 4 + [IN_PLACE] * len(after)
    args = [own, first, side, second, *after]
    aliases = {}
    if out is not None:
        in_specs.append(IN_HBM)
        args.append(out)
        aliases = {len(args) - 1: 0}
    return pl.pallas_call(
        functools.partial(finish_kernel, offset),
        in_specs=in_specs,
        out_specs=IN_HBM,
        out_shape=jax.ShapeDtypeStruct((SEGS, steps_all, width), jnp.bfloat16),
        scratch_shapes=[
            pltpu.VMEM((2, ROLE_SEGS, steps, width), jnp.bfloat16),
            pltpu.SemaphoreType.DMA((2,)),
        ],
        input_output_aliases=aliases,
        compiler_params=params(),
        cost_estimate=cost(FINISH_US),
        name="finish",
    )(*args)


def to_chan(value, target):
    return lax.ppermute(value, "chan", [(i, target(i)) for i in range(8)])


def flip_core(i):
    return i ^ 1


def mate(i):
    return i ^ 2 if i % 2 == 0 else 2 * (3 - i // 2) + 1


def face(i):
    return 2 * (3 - i // 2) if i % 2 == 0 else i ^ 2


def mate_across(i):
    return mate(i ^ 1)


def face_across(i):
    return face(i) ^ 1


def face_other_role(i):
    return face(i ^ 1)


def along_y(value, by):
    return lax.ppermute(
        value, "seq", [(s, s // 4 * 4 + (s % 4 + by) % 4) for s in range(16)]
    )


def around_z(value):
    return lax.ppermute(value, "seq", [(s, (s + 4) % 16) for s in range(16)])


def blocks_decay(rate_ref, block_rows, count):
    return jnp.exp(-rate_ref[...] * (float(block_rows) * count))


def pair_kernel(block_rows, bit, rate_ref, mine_ref, theirs_ref, *refs):
    total_ref, ahead_ref = refs[-2:]
    z, y, chip, core = position()
    second = lax.rem(y if bit == 0 else z, 2) == 1
    mine, theirs = mine_ref[...], theirs_ref[...]
    decay = blocks_decay(rate_ref, block_rows, 1.0)
    total_ref[...] = jnp.where(second, mine + decay * theirs, decay * mine + theirs)
    ahead_ref[...] = jnp.where(second, theirs, 0.0)


def quad_kernel(block_rows, bit, last, rate_ref, mine_ref, theirs_ref, ahead_ref, *refs):
    z, y, chip, core = position()
    at = y if bit == 0 else z
    theirs = theirs_ref[...]
    parity = lax.rem(at, 2).astype(jnp.float32)
    ahead = ahead_ref[...] + jnp.where(
        at >= 2, blocks_decay(rate_ref, block_rows, parity) * theirs, 0.0
    )
    if last:
        row_ahead_ref, out_ref = refs[0], refs[-1]
        within = blocks_decay(rate_ref, block_rows // 4, y.astype(jnp.float32))
        out_ref[...] = row_ahead_ref[...] + within * ahead
    else:
        total_ref, out_ref = refs[-2:]
        mine = mine_ref[...]
        decay = blocks_decay(rate_ref, block_rows, 2.0)
        total_ref[...] = jnp.where(at >= 2, mine + decay * theirs, decay * mine + theirs)
        out_ref[...] = ahead


def state_step(kernel, name, args, after, outputs):
    same = jax.ShapeDtypeStruct(args[0].shape, args[0].dtype)
    return pl.pallas_call(
        kernel,
        in_specs=[IN_VMEM] * len(args) + [IN_PLACE] * len(after),
        out_specs=[IN_VMEM] * outputs,
        out_shape=[same] * outputs,
        compiler_params=params(),
        cost_estimate=cost(ROW_US if name[0] == "r" else COLUMN_US),
        name=name,
    )(*args, *after)


def across(value, bits):
    return lax.ppermute(value, "seq", [(s, s ^ bits) for s in range(16)])


def arriving_state(closing, rate, rows, after):
    part = functools.partial
    pair, ahead = state_step(
        part(pair_kernel, rows, 0), "row_pair", [rate, closing, across(closing, 1)], after[0], 2
    )
    total, row_ahead = state_step(
        part(quad_kernel, rows, 0, False), "row_quad", [rate, pair, across(pair, 2), ahead], after[1], 2
    )
    pair, ahead = state_step(
        part(pair_kernel, 4 * rows, 1), "column_pair", [rate, total, across(total, 4)], after[2], 2
    )
    return state_step(
        part(quad_kernel, 4 * rows, 1, True), "column_quad",
        [rate, pair, across(pair, 8), ahead, row_ahead], after[3], 1,
    )[0]


PARTS = (96, 96)
SEND_US = 0.4
SIDE_US = 0.4
STACK_US = 2.0
ROW_US = 3.5
COLUMN_US = 1.0
FINISH_US = 0.4
OWN_US = 0.8


def shards(gate_query, key_proj, value_proj, decay_rates, residues, skip_weight, out_weight):
    rows_here, width_here = key_proj.shape
    steps_all = rows_here // SEGS
    weight = out_weight.reshape(8, width_here, width_here)
    p, entry, closing, rate, *pieces = closing_pass(key_proj, value_proj, decay_rates, weight)
    for_sibling, quarters = pieces[:4], pieces[4:]
    first_quarter = to_chan(quarters[0], face)
    second_quarter = to_chan(quarters[1], face_other_role)
    sibling = [to_chan(piece, flip_core) for piece in for_sibling]
    quarter = merge(first_quarter, second_quarter, [])
    waits = [[], [], [first_quarter], [sibling[0], second_quarter]]
    arriving = arriving_state(closing, rate, rows_here, waits)
    quarter_after = merge(first_quarter, second_quarter, [arriving])
    pieces = [quarter, along_y(quarter, 1), around_z(quarter_after), along_y(quarter, 3)]
    gain = residues * jnp.sqrt(-jnp.expm1(-2.0 * decay_rates))

    starts = [sum(PARTS[:part]) for part in range(len(PARTS))]
    count = len(PARTS)
    state = entry
    blocks = []
    for part, steps in enumerate(PARTS):
        mine, other, state = gate_pass(
            p, gate_query, rate, gain, skip_weight, state,
            arriving if part == 0 else None, starts[part], steps,
            [blocks[0][2]] if part == 1 else [],
        )
        blocks.append(
            [mine, to_chan(mine, mate), to_chan(other, flip_core), to_chan(other, mate_across)]
        )
    facing = stack_blocks(pieces, [])
    firsts, seconds = [], []
    sides = [side_products(blocks[0], sibling, [])]
    for part in range(count):
        first, second = send_products(blocks[part], facing, [sides[part]])
        firsts.append(to_chan(first, face))
        seconds.append(to_chan(second, face_across))
        if part + 1 < count:
            sides.append(side_products(blocks[part + 1], sibling, [first]))
    sides = [to_chan(side, flip_core) for side in sides]
    owns = [own_products(blocks[part], weight, [first]) for part in range(count)]
    out = None
    for part in range(count):
        out = finish(
            owns[part], firsts[part], sides[part], seconds[part], out, starts[part], steps_all, []
        )
    return out.reshape(rows_here, width_here)


def solution(mesh):
    in_specs = (
        P("seq", "chan"),
        P("seq", "chan"),
        P("seq", "chan"),
        P(None, "chan"),
        P(None, "chan"),
        P("chan"),
        P(None, "chan"),
    )
    out_specs = P("seq", "chan")
    return jax.shard_map(shards, mesh=mesh, in_specs=in_specs, out_specs=out_specs, check_vma=False)
```

```python
import functools

import jax
import jax.numpy as jnp
from jax import lax
from jax.experimental import pallas as pl
from jax.experimental.pallas import tpu as pltpu
from jax.sharding import PartitionSpec as P

SEGS = 8
ROLE_SEGS = 4
LANES = 128
LOADS = 4
IN_VMEM = pl.BlockSpec(memory_space=pltpu.VMEM)
IN_SMEM = pl.BlockSpec(memory_space=pltpu.SMEM)
IN_PLACE = pl.BlockSpec(memory_space=pl.ANY)
IN_HBM = pl.BlockSpec(memory_space=pltpu.HBM)


def params(mebibytes=8):
    return pltpu.CompilerParams(vmem_limit_bytes=mebibytes << 20)


def in_hbm(value):
    return pltpu.with_memory_space_constraint(value, pltpu.HBM)


def position():
    seq, chan = lax.axis_index("seq"), lax.axis_index("chan")
    return lax.div(seq, 4), lax.rem(seq, 4), lax.div(chan, 2), lax.rem(chan, 2)


def mate_chip(chip, core):
    return jnp.where(core == 0, jnp.bitwise_xor(chip, 1), 3 - chip)


def face_chip(chip, core):
    return jnp.where(core == 0, 3 - chip, jnp.bitwise_xor(chip, 1))


def depth_block(chip, core, k):
    at_chip = jnp.where(k % 2 == 1, mate_chip(chip, core), chip)
    return 2 * at_chip + jnp.bitwise_xor(core, k // 2)


def own_quarter():
    z, y, chip, core = position()
    return lax.rem(y + 2 * z, 4)


def cost(microseconds):
    return pl.CostEstimate(flops=int(microseconds * 1.15e9), bytes_accessed=0, transcendentals=0)


def spread(row):
    return jnp.broadcast_to(row, (SEGS, LANES))


def tiles(width):
    return [slice(at, at + LANES) for at in range(0, width, LANES)]


def closing_kernel(
    k_hbm, v_hbm, rate_hbm, weight_hbm, p_ref, entry_ref, closing_ref, rate_ref,
    sib0_ref, sib1_ref, sib2_ref, sib3_ref,
    first_ref, second_ref, k_buf, v_buf, flat_ref, state_ref, sems, other_sems,
):
    modes, width = rate_ref.shape
    steps = p_ref.shape[0]
    span = steps // LOADS
    stride = span + 1
    rate_copy = pltpu.make_async_copy(rate_hbm, rate_ref, other_sems.at[0])
    rate_copy.start()
    copies = []
    for i in range(LOADS):
        here = pl.ds(i * span, span)
        pair = [
            pltpu.make_async_copy(src.at[:, here, :], buf.at[i], sems.at[which, i])
            for which, (src, buf) in enumerate(((k_hbm, k_buf), (v_hbm, v_buf)))
        ]
        for copy in pair:
            copy.start()
        copies.append(pair)
    z, y, chip, core = position()
    weight_copies = [
        pltpu.make_async_copy(
            weight_hbm.at[depth_block(chip, 1 - core, k)], out_ref, other_sems.at[1 + k]
        )
        for k, out_ref in enumerate((sib0_ref, sib1_ref, sib2_ref, sib3_ref))
    ]
    quarter = own_quarter()
    for i, out_ref in enumerate((first_ref, second_ref)):
        target = jnp.bitwise_xor(core, i)
        target_chip = face_chip(chip, target)
        at_chip = jnp.where(lax.rem(quarter, 2) == 1, mate_chip(target_chip, target), target_chip)
        block = 2 * at_chip + jnp.bitwise_xor(target, lax.div(quarter, 2))
        weight_copies.append(
            pltpu.make_async_copy(weight_hbm.at[block], out_ref, other_sems.at[5 + i])
        )
    for copy in weight_copies:
        copy.start()
    rate_copy.wait()
    rate = rate_ref[...]
    pole = jnp.exp(-rate)
    turns = [(i, cols) for i in range(LOADS) for cols in tiles(width)]

    def multiply(turn):
        i, cols = turns[turn]
        if turn % (width // LANES) == 0:
            for copy in copies[i]:
                copy.wait()
        for s in range(SEGS):
            flat_ref[turn % 2, s * stride : s * stride + span, :] = k_buf[i, s, :, cols].astype(
                jnp.float32
            ) * v_buf[i, s, :, cols].astype(jnp.float32)

    multiply(0)
    for turn, (i, cols) in enumerate(turns):
        if turn + 1 < len(turns):
            multiply(turn + 1)
        poles = [spread(pole[m : m + 1, cols]) for m in range(modes)]
        if i == 0:
            states = [jnp.zeros((SEGS, LANES), jnp.float32)] * modes
        else:
            states = [state_ref[m, :, cols] for m in range(modes)]
        for t in range(span):
            x = flat_ref[turn % 2, pl.ds(t, SEGS, stride=stride), :]
            p_ref[i * span + t, :, cols] = x
            states = [a * s + x for a, s in zip(poles, states)]
        for m in range(modes):
            state_ref[m, :, cols] = states[m]
    once = jnp.exp(-rate * steps)
    twice = once * once
    hops = ((1, once), (2, twice), (4, twice * twice))
    segment = lax.broadcasted_iota(jnp.int32, (SEGS, LANES), 0)
    for cols in tiles(width):
        for m in range(modes):
            total = state_ref[m, :, cols]
            for hop, decay in hops:
                moved = jnp.where(segment >= hop, pltpu.roll(total, hop, 0), 0.0)
                total = total + spread(decay[m : m + 1, cols]) * moved
            entry_ref[m, :, cols] = jnp.where(segment >= 1, pltpu.roll(total, 1, 0), 0.0)
            closing_ref[m : m + 1, cols] = total[SEGS - 1 :, :]
    for copy in weight_copies:
        copy.wait()


CLOSING_GRANT = 12
CLOSING_US = 1.0
MERGE_US = 0.4
GATE_US = 0.8
UNROLL_GATE = 16


def merge_kernel(first_ref, second_ref, *refs):
    out_ref = refs[-1]
    width = first_ref.shape[1]
    out_ref[:, :width] = first_ref[...]
    out_ref[:, width:] = second_ref[...]


def merge(first, second, after):
    return pl.pallas_call(
        merge_kernel,
        in_specs=[IN_VMEM] * 2 + [IN_PLACE] * len(after),
        out_specs=IN_VMEM,
        out_shape=jax.ShapeDtypeStruct((first.shape[0], 2 * first.shape[1]), first.dtype),
        compiler_params=params(),
        cost_estimate=cost(MERGE_US),
        name="merge",
    )(first, second, *after)


def closing_pass(k, v, rate, weight):
    rows, width = k.shape
    modes = rate.shape[0]
    steps = rows // SEGS
    span = steps // LOADS
    buffer = pltpu.VMEM((LOADS, SEGS, span, width), k.dtype)
    return pl.pallas_call(
        closing_kernel,
        in_specs=[IN_HBM] * 4,
        out_specs=[IN_VMEM] * 10,
        out_shape=[
            jax.ShapeDtypeStruct((steps, SEGS, width), jnp.float32),
            jax.ShapeDtypeStruct((modes, SEGS, width), jnp.float32),
            jax.ShapeDtypeStruct((modes, width), jnp.float32),
            jax.ShapeDtypeStruct((modes, width), jnp.float32),
        ]
        + [jax.ShapeDtypeStruct(weight.shape[1:], weight.dtype)] * 6,
        scratch_shapes=[
            buffer,
            buffer,
            pltpu.VMEM((2, SEGS * (span + 1), LANES), jnp.float32),
            pltpu.VMEM((modes, SEGS, width), jnp.float32),
            pltpu.SemaphoreType.DMA((2, LOADS)),
            pltpu.SemaphoreType.DMA((7,)),
        ],
        compiler_params=params(CLOSING_GRANT),
        cost_estimate=cost(CLOSING_US),
        name="closing_pass",
    )(
        in_hbm(k.reshape(SEGS, steps, width)),
        in_hbm(v.reshape(SEGS, steps, width)),
        in_hbm(rate),
        in_hbm(weight),
    )


def gate_kernel(first, waits, offset, p_ref, q_hbm, rate_ref, gain_ref, skip_ref, *rest):
    arriving_ref = rest[0]
    entry_ref = rest[int(first)]
    mine_ref, other_ref, after_ref, flat_ref, q_buf, sem = rest[int(first) + 1 + waits :]
    modes, width = rate_ref.shape
    steps = mine_ref.shape[0] // ROLE_SEGS
    stride = steps + 1
    fetch = pltpu.make_async_copy(q_hbm.at[:, pl.ds(offset, steps), :], q_buf, sem)
    fetch.start()
    rate = rate_ref[...]
    pole = jnp.exp(-rate)
    if first:
        once = jnp.exp(-rate * p_ref.shape[0])
        twice = once * once
        fourth = twice * twice
        segment = lax.broadcasted_iota(jnp.int32, (SEGS, LANES), 0)
        odd, upper, top = (segment % 2 >= 1, segment % 4 >= 2, segment >= 4)
    for at, cols in enumerate(tiles(width)):
        poles = [spread(pole[m : m + 1, cols]) for m in range(modes)]
        gains = [spread(gain_ref[m : m + 1, cols]) for m in range(modes)]
        skip = spread(skip_ref[:, cols])
        states = []
        for m in range(modes):
            state = entry_ref[m, :, cols]
            if first:
                carried = spread(arriving_ref[m : m + 1, cols])
                for picked, decay in ((odd, once), (upper, twice), (top, fourth)):
                    carried = jnp.where(picked, carried * spread(decay[m : m + 1, cols]), carried)
                state = state + carried
            states.append(state)

        def step(t, states):
            x = p_ref[offset + t, :, cols]
            states = tuple(a * s + x for a, s in zip(poles, states))
            terms = [g * s for g, s in zip(gains, states)] + [skip * x]
            while len(terms) > 1:
                terms = [
                    terms[i] + terms[i + 1] if i + 1 < len(terms) else terms[i]
                    for i in range(0, len(terms), 2)
                ]
            flat_ref[at, pl.ds(t, SEGS, stride=stride), :] = terms[0]
            return states

        states = lax.fori_loop(0, steps, step, tuple(states), unroll=UNROLL_GATE)
        for m in range(modes):
            after_ref[m, :, cols] = states[m]
    fetch.wait()
    z, y, chip, core = position()
    for mine in (0, 1):

        @pl.when(core == mine)
        def _():
            for at, cols in enumerate(tiles(width)):
                for s in range(SEGS):
                    y = flat_ref[at, s * stride : s * stride + steps, :]
                    q = q_buf[s, :, cols].astype(jnp.float32)
                    target = mine_ref if s // ROLE_SEGS == mine else other_ref
                    rows = slice(s % ROLE_SEGS * steps, (s % ROLE_SEGS + 1) * steps)
                    target[rows, cols] = (q * y).astype(jnp.bfloat16)


def gate_pass(p, q, rate, gain, skip, entry, arriving, offset, steps, after):
    steps_all, segs, width = p.shape
    modes = rate.shape[0]
    first = arriving is not None
    args = [p, in_hbm(q.reshape(SEGS, steps_all, width)), rate, gain, skip.reshape(1, width)]
    args += ([arriving] if first else []) + [entry]
    in_specs = [IN_VMEM] * len(args) + [IN_PLACE] * len(after)
    in_specs[1] = IN_HBM
    return pl.pallas_call(
        functools.partial(gate_kernel, first, len(after), offset),
        in_specs=in_specs,
        out_specs=[IN_VMEM] * 3,
        out_shape=[
            jax.ShapeDtypeStruct((ROLE_SEGS * steps, width), jnp.bfloat16),
            jax.ShapeDtypeStruct((ROLE_SEGS * steps, width), jnp.bfloat16),
            jax.ShapeDtypeStruct((modes, SEGS, width), jnp.float32),
        ],
        scratch_shapes=[
            pltpu.VMEM((width // LANES, SEGS * (steps + 1), LANES), jnp.float32),
            pltpu.VMEM((SEGS, steps, width), q.dtype),
            pltpu.SemaphoreType.DMA,
        ],
        compiler_params=params(),
        cost_estimate=cost(GATE_US * steps / 96),
        name="gate_pass",
    )(*args, *after)


def stack_kernel(*refs):
    pieces, out_ref = refs[:4], refs[-1]
    k = own_quarter()
    for i, piece in enumerate(pieces):
        out_ref[lax.rem(k + 4 - i, 4)] = piece[...]


def stack_blocks(pieces, after):
    return pl.pallas_call(
        stack_kernel,
        in_specs=[IN_VMEM] * len(pieces) + [IN_PLACE] * len(after),
        out_specs=IN_VMEM,
        out_shape=jax.ShapeDtypeStruct((len(pieces),) + pieces[0].shape, pieces[0].dtype),
        compiler_params=params(),
        cost_estimate=cost(STACK_US),
        name="stack_blocks",
    )(*pieces, *after)


def send_kernel(*refs):
    blocks, facing_ref, (first_ref, second_ref) = refs[:4], refs[4], refs[-2:]
    width = first_ref.shape[1]
    total = jnp.dot(blocks[0][...], facing_ref[0], preferred_element_type=jnp.float32)
    for k in range(1, 4):
        total += jnp.dot(blocks[k][...], facing_ref[k], preferred_element_type=jnp.float32)
    first_ref[...] = total[:, :width].astype(first_ref.dtype)
    second_ref[...] = total[:, width:].astype(second_ref.dtype)


def send_products(blocks, facing, after):
    rows = blocks[0].shape[0]
    width = facing.shape[2] // 2
    return pl.pallas_call(
        send_kernel,
        in_specs=[IN_VMEM] * 5 + [IN_PLACE] * len(after),
        out_specs=[IN_VMEM] * 2,
        out_shape=[jax.ShapeDtypeStruct((rows, width), jnp.bfloat16)] * 2,
        compiler_params=params(),
        cost_estimate=cost(SEND_US),
        name="send_products",
    )(*blocks, facing, *after)


def side_kernel(*refs):
    blocks, weights, out_ref = refs[:4], refs[4:8], refs[-1]
    total = jnp.dot(blocks[0][...], weights[0][...], preferred_element_type=jnp.float32)
    for k in range(1, 4):
        total += jnp.dot(blocks[k][...], weights[k][...], preferred_element_type=jnp.float32)
    out_ref[...] = total.astype(out_ref.dtype)


def side_products(blocks, sibling, after):
    rows = blocks[0].shape[0]
    width = sibling[0].shape[1]
    return pl.pallas_call(
        side_kernel,
        in_specs=[IN_VMEM] * 8 + [IN_PLACE] * len(after),
        out_specs=IN_VMEM,
        out_shape=jax.ShapeDtypeStruct((rows, width), jnp.bfloat16),
        compiler_params=params(),
        cost_estimate=cost(SIDE_US),
        name="side_products",
    )(*blocks, *sibling, *after)


def own_kernel(*refs):
    blocks, weight_hbm = refs[:4], refs[4]
    out_ref, weight_buf, sems = refs[-3:]
    z, y, chip, core = position()
    fetches = [
        pltpu.make_async_copy(
            weight_hbm.at[depth_block(chip, core, k)], weight_buf.at[k], sems.at[k]
        )
        for k in range(4)
    ]
    for fetch in fetches:
        fetch.start()
    fetches[0].wait()
    total = jnp.dot(blocks[0][...], weight_buf[0], preferred_element_type=jnp.float32)
    for k in range(1, 4):
        fetches[k].wait()
        total += jnp.dot(blocks[k][...], weight_buf[k], preferred_element_type=jnp.float32)
    out_ref[...] = total


def own_products(blocks, weight, after):
    rows, depth = blocks[0].shape
    width = weight.shape[2]
    return pl.pallas_call(
        own_kernel,
        in_specs=[IN_VMEM] * 4 + [IN_HBM] + [IN_PLACE] * len(after),
        out_specs=IN_VMEM,
        out_shape=jax.ShapeDtypeStruct((rows, width), jnp.float32),
        scratch_shapes=[
            pltpu.VMEM((4, depth, width), weight.dtype),
            pltpu.SemaphoreType.DMA((4,)),
        ],
        compiler_params=params(),
        cost_estimate=cost(OWN_US),
        name="own_products",
    )(*blocks, in_hbm(weight), *after)


def finish_kernel(offset, own_ref, first_ref, side_ref, second_ref, *refs):
    out_hbm, block_ref, sem = refs[-3:]
    z, y, chip, core = position()
    here = pl.ds(offset, block_ref.shape[2])
    copies = []
    for i, (kept_ref, sent_ref) in enumerate(((own_ref, first_ref), (side_ref, second_ref))):
        total = kept_ref[...].astype(jnp.float32) + sent_ref[...].astype(jnp.float32)
        block_ref[i] = total.astype(block_ref.dtype).reshape(block_ref.shape[1:])
        segments = pl.ds(jnp.bitwise_xor(core, i) * ROLE_SEGS, ROLE_SEGS)
        copies.append(
            pltpu.make_async_copy(block_ref.at[i], out_hbm.at[segments, here, :], sem.at[i])
        )
        copies[i].start()
    for copy in copies:
        copy.wait()


def finish(own, first, side, second, out, offset, steps_all, after):
    rows, width = own.shape
    steps = rows // ROLE_SEGS
    in_specs = [IN_VMEM] * 4 + [IN_PLACE] * len(after)
    args = [own, first, side, second, *after]
    aliases = {}
    if out is not None:
        in_specs.append(IN_HBM)
        args.append(out)
        aliases = {len(args) - 1: 0}
    return pl.pallas_call(
        functools.partial(finish_kernel, offset),
        in_specs=in_specs,
        out_specs=IN_HBM,
        out_shape=jax.ShapeDtypeStruct((SEGS, steps_all, width), jnp.bfloat16),
        scratch_shapes=[
            pltpu.VMEM((2, ROLE_SEGS, steps, width), jnp.bfloat16),
            pltpu.SemaphoreType.DMA((2,)),
        ],
        input_output_aliases=aliases,
        compiler_params=params(),
        cost_estimate=cost(FINISH_US),
        name="finish",
    )(*args)


def to_chan(value, target):
    return lax.ppermute(value, "chan", [(i, target(i)) for i in range(8)])


def flip_core(i):
    return i ^ 1


def mate(i):
    return i ^ 2 if i % 2 == 0 else 2 * (3 - i // 2) + 1


def face(i):
    return 2 * (3 - i // 2) if i % 2 == 0 else i ^ 2


def mate_across(i):
    return mate(i ^ 1)


def face_across(i):
    return face(i) ^ 1


def face_other_role(i):
    return face(i ^ 1)


def along_y(value, by):
    return lax.ppermute(
        value, "seq", [(s, s // 4 * 4 + (s % 4 + by) % 4) for s in range(16)]
    )


def around_z(value):
    return lax.ppermute(value, "seq", [(s, (s + 4) % 16) for s in range(16)])


def blocks_decay(rate_ref, block_rows, count):
    return jnp.exp(-rate_ref[...] * (float(block_rows) * count))


def pair_kernel(block_rows, bit, rate_ref, mine_ref, theirs_ref, *refs):
    total_ref, ahead_ref = refs[-2:]
    z, y, chip, core = position()
    second = lax.rem(y if bit == 0 else z, 2) == 1
    mine, theirs = mine_ref[...], theirs_ref[...]
    decay = blocks_decay(rate_ref, block_rows, 1.0)
    total_ref[...] = jnp.where(second, mine + decay * theirs, decay * mine + theirs)
    ahead_ref[...] = jnp.where(second, theirs, 0.0)


def quad_kernel(block_rows, bit, last, rate_ref, mine_ref, theirs_ref, ahead_ref, *refs):
    z, y, chip, core = position()
    at = y if bit == 0 else z
    theirs = theirs_ref[...]
    parity = lax.rem(at, 2).astype(jnp.float32)
    ahead = ahead_ref[...] + jnp.where(
        at >= 2, blocks_decay(rate_ref, block_rows, parity) * theirs, 0.0
    )
    if last:
        row_ahead_ref, out_ref = refs[0], refs[-1]
        within = blocks_decay(rate_ref, block_rows // 4, y.astype(jnp.float32))
        out_ref[...] = row_ahead_ref[...] + within * ahead
    else:
        total_ref, out_ref = refs[-2:]
        mine = mine_ref[...]
        decay = blocks_decay(rate_ref, block_rows, 2.0)
        total_ref[...] = jnp.where(at >= 2, mine + decay * theirs, decay * mine + theirs)
        out_ref[...] = ahead


def state_step(kernel, name, args, after, outputs):
    same = jax.ShapeDtypeStruct(args[0].shape, args[0].dtype)
    return pl.pallas_call(
        kernel,
        in_specs=[IN_VMEM] * len(args) + [IN_PLACE] * len(after),
        out_specs=[IN_VMEM] * outputs,
        out_shape=[same] * outputs,
        compiler_params=params(),
        cost_estimate=cost(ROW_US if name[0] == "r" else COLUMN_US),
        name=name,
    )(*args, *after)


def across(value, bits):
    return lax.ppermute(value, "seq", [(s, s ^ bits) for s in range(16)])


def arriving_state(closing, rate, rows, after):
    part = functools.partial
    pair, ahead = state_step(
        part(pair_kernel, rows, 0), "row_pair", [rate, closing, across(closing, 1)], after[0], 2
    )
    total, row_ahead = state_step(
        part(quad_kernel, rows, 0, False), "row_quad", [rate, pair, across(pair, 2), ahead], after[1], 2
    )
    pair, ahead = state_step(
        part(pair_kernel, 4 * rows, 1), "column_pair", [rate, total, across(total, 4)], after[2], 2
    )
    return state_step(
        part(quad_kernel, 4 * rows, 1, True), "column_quad",
        [rate, pair, across(pair, 8), ahead, row_ahead], after[3], 1,
    )[0]


PARTS = (96, 96)
SEND_US = 0.4
SIDE_US = 0.4
STACK_US = 2.0
ROW_US = 3.5
COLUMN_US = 1.0
FINISH_US = 0.4
OWN_US = 0.8


def shards(gate_query, key_proj, value_proj, decay_rates, residues, skip_weight, out_weight):
    rows_here, width_here = key_proj.shape
    steps_all = rows_here // SEGS
    weight = out_weight.reshape(8, width_here, width_here)
    p, entry, closing, rate, *pieces = closing_pass(key_proj, value_proj, decay_rates, weight)
    for_sibling, quarters = pieces[:4], pieces[4:]
    first_quarter = to_chan(quarters[0], face)
    second_quarter = to_chan(quarters[1], face_other_role)
    sibling = [to_chan(piece, flip_core) for piece in for_sibling]
    quarter = merge(first_quarter, second_quarter, [])
    waits = [[], [], [first_quarter], [sibling[0], second_quarter]]
    arriving = arriving_state(closing, rate, rows_here, waits)
    quarter_after = merge(first_quarter, second_quarter, [arriving])
    pieces = [quarter, along_y(quarter, 1), around_z(quarter_after), along_y(quarter, 3)]
    gain = residues * jnp.sqrt(-jnp.expm1(-2.0 * decay_rates))

    starts = [sum(PARTS[:part]) for part in range(len(PARTS))]
    count = len(PARTS)
    state = entry
    blocks = []
    for part, steps in enumerate(PARTS):
        mine, other, state = gate_pass(
            p, gate_query, rate, gain, skip_weight, state,
            arriving if part == 0 else None, starts[part], steps,
            [blocks[0][2]] if part == 1 else [],
        )
        blocks.append(
            [mine, to_chan(mine, mate), to_chan(other, flip_core), to_chan(other, mate_across)]
        )
    facing = stack_blocks(pieces, [])
    firsts, seconds = [], []
    sides = [side_products(blocks[0], sibling, [])]
    for part in range(count):
        first, second = send_products(blocks[part], facing, [sides[part]])
        firsts.append(to_chan(first, face))
        seconds.append(to_chan(second, face_across))
        if part + 1 < count:
            sides.append(side_products(blocks[part + 1], sibling, [first]))
    sides = [to_chan(side, flip_core) for side in sides]
    owns = [own_products(blocks[part], weight, [first]) for part in range(count)]
    out = None
    for part in range(count):
        out = finish(
            owns[part], firsts[part], sides[part], seconds[part], out, starts[part], steps_all, []
        )
    return out.reshape(rows_here, width_here)


def solution(mesh):
    in_specs = (
        P("seq", "chan"),
        P("seq", "chan"),
        P("seq", "chan"),
        P(None, "chan"),
        P(None, "chan"),
        P("chan"),
        P(None, "chan"),
    )
    out_specs = P("seq", "chan")
    return jax.shard_map(shards, mesh=mesh, in_specs=in_specs, out_specs=out_specs, check_vma=False)
```
